768 devices in a mesh: row: 192 (over y, z, core), col: 4 (over x).
Axes of the slice: x: 4, y: 8, z: 12, core: 2. Of those that a mesh axis runs over, the one named last changes fastest.
Arguments:
- amplitudes: bfloat16 [96, 576, 2500], P(None, 'row'), may hold values from -6 to 6
- integrals: bfloat16 [3072, 200, 2500], P(('row', 'col')), may hold values from -0.125 to 0.125
- cd_tile: int32 [4], replicated, may hold values from 0 to 95
- target: int32 [3072], replicated, may hold values from 0 to 3
- counts: int32 [768], replicated, may hold values from 1 to 4, as said below
Outputs:
- residual: float32 [768, 576, 200], P(('row', 'col'))
The draws below stay inside these ranges and needn't reach their ends.
Inputs may be any that keep to these rules, and one draw needn't show every extreme that they name: `counts`: some device has 4 live slots.
All inputs are finite; a program needn't handle non-finite values.
Results may differ from the reference program's by a relative error of at most 0.0003.
Values may be sent and summed in bfloat16 or wider, within the bound.
A program may use at most 64 MiB of HBM per device.

```python
import jax
import jax.numpy as jnp
from jax import lax

P_SIZE = 576
TP = 2500
CDW = 96
RB = 200
K_DEV = 4
BLK_DEV = 1
PIECES = 3072
N_ROW = 192
N_COL = 4
DEVICES = 768


def draw_counts(key, part):
    key = jax.random.fold_in(key, 7)
    first, second = jax.random.split(key)
    heavy = jax.random.randint(first, (DEVICES,), 0, 4)
    light = jax.random.randint(second, (DEVICES,), 0, K_DEV)
    values = jnp.where(heavy == 0, K_DEV, 1 + light // 2)
    return values.at[0].set(K_DEV).astype(jnp.int32)


def with_ends(entries, key, low, largest):
    longest = entries.shape.index(max(entries.shape))
    spots = []
    for shift in (0, 1):
        where = [jax.random.randint(jax.random.fold_in(key, axis), (), 0, length) for axis, length in enumerate(entries.shape)]
        where[longest] = (where[longest] + shift) % entries.shape[longest]
        spots.append(tuple(where))
    return entries.at[spots[0]].set(low).at[spots[1]].set(largest)


def levels(stream_key, extent, cuts, smallest, largest):
    loudness, own = 1.0, jax.random.fold_in(stream_key, 6)
    for position, shards_of in cuts:
        draws = jnp.exp(jax.random.uniform(jax.random.fold_in(own, position), (shards_of,), jnp.float32, smallest / len(cuts), largest / len(cuts)))
        loudness = loudness * jnp.repeat(draws, extent[position] // shards_of).reshape([-1 if axis == position else 1 for axis in range(len(extent))])
    return loudness


def bell_draw(stream_key, shape, spread, reach, cuts=(), kind=jnp.bfloat16):
    values = jax.random.normal(stream_key, shape, jnp.float32) * spread
    if len(cuts) > 0:
        values = levels(stream_key, shape, cuts, -0.22, 0.18) * values
    return jnp.clip(values, min=-reach, max=reach).astype(kind)


def setup_inputs(seed: int = 0) -> dict:
    seeds = jax.random.split(jax.random.key(seed), 6)
    return {
        "amplitudes": bell_draw(seeds[0], (CDW, P_SIZE, TP), 1.0, 6.0, ((1, 192),)),
        "integrals": bell_draw(seeds[1], (PIECES, RB, TP), TP ** -0.5, 0.125, ((0, 768),)),
        "cd_tile": with_ends(jax.random.randint(seeds[2], (N_COL,), 0, CDW), jax.random.fold_in(seeds[2], 1), 0, CDW - 1).astype(jnp.int32),
        "target": with_ends(jax.random.randint(seeds[3], (PIECES,), 0, BLK_DEV * N_COL), jax.random.fold_in(seeds[3], 1), 0, (BLK_DEV * N_COL) - 1).astype(jnp.int32),
        "counts": draw_counts(jax.random.fold_in(seeds[5], 71), 0),
    }


def reference(amplitudes, integrals, cd_tile, target, counts):
    total = BLK_DEV * N_ROW * N_COL

    def step(index, output):
        device = index // K_DEV
        slot_id = index % K_DEV
        column = device % N_COL
        tile_pair = cd_tile[column]
        amp_tile = lax.dynamic_index_in_dim(amplitudes, tile_pair, 0, keepdims=False).astype(jnp.float32)
        piece = lax.dynamic_index_in_dim(integrals, index, 0, keepdims=False).astype(jnp.float32)
        term = jnp.dot(amp_tile, piece.T, precision=lax.Precision.HIGHEST)
        live = slot_id < counts[device]
        term = jnp.where(live, term, jnp.zeros_like(term))
        block = ((device // N_COL) * (N_COL * BLK_DEV) + target[index]).astype(jnp.int32)
        current = lax.dynamic_index_in_dim(output, block, 0, keepdims=False)
        return lax.dynamic_update_index_in_dim(output, current + term, block, 0)

    start = jnp.zeros((total, P_SIZE, RB), jnp.float32)
    return lax.fori_loop(jnp.int32(0), jnp.int32(PIECES), step, start)
```

```python
import jax
import jax.numpy as jnp
from jax import lax
from jax.experimental import pallas as pl
from jax.experimental.pallas import tpu as pltpu
from jax.sharding import PartitionSpec as P

MESH = pl.DeviceIdType.MESH
NY, NZ, NX = 8, 12, 4
ROWS = 3
KT = 20
TP = 2500
CDW = 96
PAIRS = 576
RB = 200
SLOTS = 4
SLAB = 128
SLABS = 5
TOP = 104
NT = (((1,), (1,)), ((), ()))


def block_order():
    order = []
    row = 0
    for half, index in (
        [(1, 0), (1, 1), (1, 2), (0, 0), (1, 3), (1, 4), (0, 1), (0, 2), (1, 5), (1, 6), (1, 7), (1, 8)]
        + [(0, 3), (0, 4), (1, 9), (1, 10), (1, 11), (0, 5), (0, 6), (0, 7)]
    ):
        order.append((half, index, row))
        row += 36 if half == 0 else 24
    return order


def distance(index):
    return -((index + 1) // 2) if index % 2 else index // 2


def kernel(
    cd_ref, target_ref, counts_ref, amp_hbm, int_hbm, out_ref,
    amp_v, int_v, shard_v, g0, g1, wide, a_f, a_b, perm, pidx,
    p_own, p_send, r_half_l, r_half_r, r_full_l, r_full_r,
    load_sem, p1_send, p1_recv, p2_send, p2_recv, sib_send, sib_recv, x_send, x_recv,
):
    row, col = lax.axis_index("row"), lax.axis_index("col")
    y, z, core = row // (2 * NZ), (row // 2) % NZ, row % 2

    def at(yy, zz, cc):
        return ((yy * NZ + zz) * 2 + cc, col)

    up, down = (y + 1) % NY, (y + NY - 1) % NY
    fwd, back = (z + 1) % NZ, (z + NZ - 1) % NZ
    right, left = (col + 1) % NX, (col + NX - 1) % NX
    sibling = at(y, z, 1 - core)
    y_up, y_down = at(up, z, core), at(down, z, core)
    z_up, z_down = at(y, fwd, core), at(y, back, core)
    x_right, x_left = (row, right), (row, left)

    load_amp = pltpu.make_async_copy(amp_hbm, amp_v, load_sem.at[0])
    load_int = pltpu.make_async_copy(int_hbm, int_v, load_sem.at[1])
    load_amp.start()
    load_int.start()

    barrier = pltpu.get_barrier_semaphore()
    for other in (sibling, y_up, y_down, z_up, z_down, x_right, x_left):
        pl.semaphore_signal(barrier, inc=1, device_id=other, device_id_type=MESH)

    shard_v[...] = jnp.zeros_like(shard_v)
    apart = jnp.abs(lax.broadcasted_iota(jnp.int32, (16, CDW), 1) - cd_ref[col])
    one_hot = (1 - jnp.minimum(apart, 1)).astype(jnp.float32).astype(jnp.bfloat16)
    load_amp.wait()
    for p in range(ROWS):
        line = jnp.dot(one_hot, amp_v[p], preferred_element_type=jnp.float32)
        for k in range(KT):
            width = min(128, TP - 128 * k)
            shard_v[p * KT + k : p * KT + k + 1, 0:width] = line[0:1, 128 * k : 128 * k + width]
    packed = shard_v[...].astype(jnp.bfloat16)

    @pl.when(core == 0)
    def _():
        g0[y, z] = packed

    @pl.when(core == 1)
    def _():
        g1[z, y] = packed

    pl.semaphore_wait(barrier, 7)

    def copy(src, dst, send, recv, device):
        return pltpu.make_async_remote_copy(
            src_ref=src, dst_ref=dst, send_sem=send, recv_sem=recv, device_id=device, device_id_type=MESH
        )

    def ring1(buf, place, n, me, ahead, behind):
        def step(s, sign):
            i = (me - sign * (s - 1) + n) % n
            ref = buf.at[place(i)]
            d = 0 if sign > 0 else 1
            return copy(ref, ref, p1_send.at[d, s - 1], p1_recv.at[d, s - 1], ahead if sign > 0 else behind)

        for s in range(1, n // 2 + 1):
            step(s, 1).start()
            if s < n // 2:
                step(s, -1).start()
            step(s, 1).wait_recv()
            if s < n // 2:
                step(s, -1).wait_recv()
        for s in range(1, n // 2 + 1):
            step(s, 1).wait_send()
            if s < n // 2:
                step(s, -1).wait_send()

    def ring2(buf, n, me, inner, ahead, behind):
        def step(s, sign):
            i = (me - sign * (s - 1) + n) % n
            d = 0 if sign > 0 else 1
            ref = buf.at[i]
            if s == n // 2:
                ref = ref.at[pl.ds(0 if sign > 0 else inner // 2, inner // 2)]
            return copy(ref, ref, p2_send.at[d, s - 1], p2_recv.at[d, s - 1], ahead if sign > 0 else behind)

        return step

    y_step = ring2(g0, NY, y, NZ, y_up, y_down)
    z_step = ring2(g1, NZ, z, NY, z_up, z_down)

    def block_at(half, index):
        n, me = (NY, y) if half == 0 else (NZ, z)
        return (me + distance(index) + n) % n

    def to_sibling(half, index):
        ref = (g0 if half == 0 else g1).at[block_at(half, index)]
        return copy(ref, ref, sib_send.at[index], sib_recv.at[index], sibling)

    @pl.when(core == 0)
    def _():
        ring1(g0, lambda i: (y, i), NZ, z, z_up, z_down)
        y_step(1, 1).start()
        y_step(1, -1).start()
        to_sibling(0, 0).start()

    @pl.when(core == 1)
    def _():
        ring1(g1, lambda i: (z, i), NY, y, y_up, y_down)
        z_step(1, 1).start()
        z_step(1, -1).start()
        to_sibling(1, 0).start()

    def arrive(half, s):
        n, step = (NY, y_step) if half == 0 else (NZ, z_step)

        @pl.when(core == half)
        def _():
            for sign in (1, -1):
                step(s, sign).wait_recv()
                if s < n // 2:
                    step(s + 1, sign).start()
                    to_sibling(half, 2 * s - (1 if sign > 0 else 0)).start()
            if s == n // 2:
                to_sibling(half, 2 * s - 1).start()

    device = row * NX + col
    count = counts_ref[device]
    weights = []
    for d in range(NX):
        owner = (col + d) % NX
        line = []
        for q in range(SLOTS):
            live = jnp.minimum(jnp.maximum(count - q, 0), 1)
            same = 1 - jnp.minimum(jnp.abs(target_ref[device * SLOTS + q] - owner), 1)
            line.append((live * same).astype(jnp.float32))
        weights.append(line)

    order = block_order()
    pidx[...] = jnp.full_like(pidx, -1)
    for half, index, first in order:
        if half == 0:
            for r in range(ROWS):
                step = lax.broadcasted_iota(jnp.int32, (NZ, 128), 0)
                pidx[first + NZ * r : first + NZ * r + NZ, :] = block_at(0, index) * 72 + r + 6 * step
        else:
            for r in range(ROWS):
                step = lax.broadcasted_iota(jnp.int32, (NY, 128), 0)
                pidx[first + NY * r : first + NY * r + NY, :] = block_at(1, index) * 6 + 3 + r + 72 * step
    for t in range(SLABS):
        lanes = lax.broadcasted_iota(jnp.int32, (SLAB * SLABS, 128), 1) + 128 * t
        perm[:, 128 * t : 128 * t + 128] = jnp.where(pidx[...] == lanes, 1.0, 0.0).astype(jnp.bfloat16)
    a_f[:, PAIRS:, :] = jnp.zeros((KT, SLAB * SLABS - PAIRS, 128), jnp.float32)

    def unpack(half, index, first):
        n = NZ if half == 0 else NY
        i = block_at(half, index)

        @pl.when(core != half)
        def _():
            to_sibling(half, index).wait_recv()

        block = (g0 if half == 0 else g1)[i]
        wide[0 : n * 64, :] = block.reshape(n * 64, 128).astype(jnp.float32)

        @pl.loop(0, KT)
        def _(k):
            for r in range(ROWS):
                a_f[k, first + n * r : first + n * r + n, :] = wide[pl.ds(r * KT + k, n, stride=64), :]

    def x_copy(j, i):
        lo, hi = pl.ds(0, TOP), pl.ds(TOP, RB - TOP)
        src, dst = [
            (p_send.at[1, j, lo], r_half_l.at[j]),
            (p_send.at[1, j, hi], r_half_r.at[j]),
            (p_send.at[0, j, hi], r_full_l.at[j, hi]),
            (p_send.at[2, j, lo], r_full_r.at[j, lo]),
            (p_send.at[0, j, lo], r_full_l.at[j, lo]),
            (p_send.at[2, j, hi], r_full_r.at[j, hi]),
        ][i]
        return copy(src, dst, x_send.at[j, i], x_recv.at[j, i], x_left if i % 2 else x_right)

    def slab(j):
        for k in range(KT):
            a_b[:, 128 * k : 128 * k + 128] = a_f[k, SLAB * j : SLAB * j + SLAB, :].astype(jnp.bfloat16)
        terms = [
            lax.dot_general(int_v[q], a_b[:, 0:TP], NT, preferred_element_type=jnp.float32) for q in range(SLOTS)
        ]

        def part(d):
            return sum(w * t for w, t in zip(weights[d], terms))

        p_send[1, j] = part(2)
        x_copy(j, 0).start()
        x_copy(j, 1).start()
        p_send[0, j] = part(1)
        x_copy(j, 2).start()
        p_send[2, j] = part(3)
        x_copy(j, 3).start()
        p_own[j] = part(0)

    def relay(j):
        x_copy(j, 0).wait_recv()
        p_send[0, j, 0:TOP] = p_send[0, j, 0:TOP] + r_half_l[j]
        x_copy(j, 4).start()
        x_copy(j, 1).wait_recv()
        p_send[2, j, TOP:RB] = p_send[2, j, TOP:RB] + r_half_r[j]
        x_copy(j, 5).start()

    def finish(j):
        for i in range(2, 6):
            x_copy(j, i).wait_recv()
        whole = p_own[j] + r_full_l[j] + r_full_r[j]
        high = whole.astype(jnp.bfloat16)
        low = (whole - high.astype(jnp.float32)).astype(jnp.bfloat16)
        mine = perm[SLAB * j : SLAB * j + SLAB, 0:PAIRS]
        more = jnp.dot(high, mine, preferred_element_type=jnp.float32)
        more = more + jnp.dot(low, mine, preferred_element_type=jnp.float32)
        if j == 0:
            out_ref[...] = more
        else:
            out_ref[...] = out_ref[...] + more

    at_row = {(h, i): f for h, i, f in order}

    def take(*blocks):
        for b in blocks:
            unpack(*b, at_row[b])

    take((1, 0))
    arrive(1, 1)
    take((1, 1), (1, 2))
    take((0, 0))
    arrive(0, 1)
    arrive(1, 2)
    take((1, 3), (1, 4))
    load_int.wait()
    slab(0)
    arrive(0, 2)
    arrive(1, 3)
    take((0, 1), (0, 2))
    take((1, 5), (1, 6))
    slab(1)
    relay(0)
    arrive(1, 4)
    take((1, 7), (1, 8))
    arrive(0, 3)
    take((0, 3), (0, 4))
    arrive(1, 5)
    slab(2)
    relay(1)
    arrive(1, 6)
    arrive(0, 4)
    take((1, 9), (1, 10), (1, 11))
    take((0, 5), (0, 6))
    slab(3)
    relay(2)
    take((0, 7))
    slab(4)
    relay(3)
    finish(0)
    finish(1)
    relay(4)
    finish(2)
    finish(3)
    finish(4)

    @pl.when(core == 0)
    def _():
        for s in range(1, NY // 2 + 1):
            y_step(s, 1).wait_send()
            y_step(s, -1).wait_send()
        for index in range(NY):
            to_sibling(0, index).wait_send()

    @pl.when(core == 1)
    def _():
        for s in range(1, NZ // 2 + 1):
            z_step(s, 1).wait_send()
            z_step(s, -1).wait_send()
        for index in range(NZ):
            to_sibling(1, index).wait_send()

    for j in range(SLABS):
        for i in range(6):
            x_copy(j, i).wait_send()


def local(amplitudes, integrals, cd_tile, target, counts):
    amp = jnp.transpose(amplitudes, (1, 0, 2))
    anywhere, scalars = pl.BlockSpec(memory_space=pl.ANY), pl.BlockSpec(memory_space=pltpu.SMEM)
    dma = pltpu.SemaphoreType.DMA
    residual = pl.pallas_call(
        kernel,
        out_shape=jax.ShapeDtypeStruct((RB, PAIRS), jnp.float32),
        in_specs=[scalars, scalars, scalars, anywhere, anywhere],
        out_specs=pl.BlockSpec(memory_space=pltpu.VMEM),
        scratch_shapes=[
            pltpu.VMEM(amp.shape, jnp.bfloat16),
            pltpu.VMEM(integrals.shape, jnp.bfloat16),
            pltpu.VMEM((64, 128), jnp.float32),
            pltpu.VMEM((NY, NZ, 64, 128), jnp.bfloat16),
            pltpu.VMEM((NZ, NY, 64, 128), jnp.bfloat16),
            pltpu.VMEM((NZ * 64, 128), jnp.float32),
            pltpu.VMEM((KT, SLAB * SLABS, 128), jnp.float32),
            pltpu.VMEM((SLAB, KT * 128), jnp.bfloat16),
            pltpu.VMEM((SLAB * SLABS, SLAB * SLABS), jnp.bfloat16),
            pltpu.VMEM((SLAB * SLABS, 128), jnp.int32),
            pltpu.VMEM((SLABS, RB, SLAB), jnp.float32),
            pltpu.VMEM((3, SLABS, RB, SLAB), jnp.float32),
            pltpu.VMEM((SLABS, TOP, SLAB), jnp.float32),
            pltpu.VMEM((SLABS, RB - TOP, SLAB), jnp.float32),
            pltpu.VMEM((SLABS, RB, SLAB), jnp.float32),
            pltpu.VMEM((SLABS, RB, SLAB), jnp.float32),
            dma((2,)),
            dma((2, 6)),
            dma((2, 6)),
            dma((2, 6)),
            dma((2, 6)),
            dma((12,)),
            dma((12,)),
            dma((SLABS, 6)),
            dma((SLABS, 6)),
        ],
        compiler_params=pltpu.CompilerParams(
            collective_id=0, has_side_effects=True, vmem_limit_bytes=56 * 1024 * 1024
        ),
        cost_estimate=pl.CostEstimate(flops=2 * SLOTS * RB * PAIRS * TP, bytes_accessed=6 * 10**6, transcendentals=0),
    )(cd_tile, target, counts, amp, integrals)
    return jnp.transpose(residual)[None]


def solution(mesh):
    in_specs = (P(None, "row", None), P(("row", "col"), None, None), P(), P(), P())
    out_specs = P(("row", "col"), None, None)
    return jax.shard_map(local, mesh=mesh, in_specs=in_specs, out_specs=out_specs, check_vma=False)
```

```python
import jax
import jax.numpy as jnp
from jax import lax
from jax.experimental import pallas as pl
from jax.experimental.pallas import tpu as pltpu
from jax.sharding import PartitionSpec as P

MESH = pl.DeviceIdType.MESH
NY, NZ, NX = 8, 12, 4
ROWS = 3
KT = 20
TP = 2500
CDW = 96
PAIRS = 576
RB = 200
SLOTS = 4
Y_REACH, Z_REACH = 2, 3
SLAB = 128
SLABS = 5
CODED = 208
LEVELS = 32000.0
NT = (((1,), (1,)), ((), ()))


def block_order():
    order = []
    row = 0
    for half, index in (
        [(1, 0), (0, 0), (1, 1), (1, 2), (1, 3), (1, 4), (0, 1), (0, 2), (1, 5), (1, 6), (0, 3), (0, 4)]
        + [(1, 7), (1, 8), (0, 5), (0, 6), (1, 9), (1, 10), (1, 11), (0, 7)]
    ):
        order.append((half, index, row))
        row += 36 if half == 0 else 24
    return order


def distance(index):
    return -((index + 1) // 2) if index % 2 else index // 2


def kernel(
    cd_ref, target_ref, counts_ref, amp_hbm, int_hbm, out_ref,
    amp_v, int_v, shard_v, g0, g1, wide, a_f, a_b, perm, pidx,
    p_own, p_send, p_got,
    load_sem, p1_send, p1_recv, p2_send, p2_recv, sib_send, sib_recv, x_send, x_recv,
):
    row, col = lax.axis_index("row"), lax.axis_index("col")
    y, z, core = row // (2 * NZ), (row // 2) % NZ, row % 2

    def at(yy, zz, cc):
        return ((yy * NZ + zz) * 2 + cc, col)

    def along_y(k):
        return at((y + k + NY) % NY, z, core)

    def along_z(k):
        return at(y, (z + k + NZ) % NZ, core)

    sibling = at(y, z, 1 - core)
    def along_x(k):
        return (row, (col + k) % NX)


    load_amp = pltpu.make_async_copy(amp_hbm, amp_v, load_sem.at[0])
    load_int = pltpu.make_async_copy(int_hbm, int_v, load_sem.at[1])
    load_amp.start()
    load_int.start()

    barrier = pltpu.get_barrier_semaphore()

    def greet(others):
        for other in others:
            pl.semaphore_signal(barrier, inc=1, device_id=other, device_id_type=MESH)

    def reach(n, r):
        return [k for s in range(r, 0, -1) for k in (s, -s)]

    greet([sibling] + [along_x(k) for k in range(1, NX)])

    @pl.when(core == 0)
    def _():
        greet([along_z(k) for k in range(1, NZ)] + [along_y(k) for k in reach(NY, Y_REACH)])

    @pl.when(core == 1)
    def _():
        greet([along_y(k) for k in range(1, NY)] + [along_z(k) for k in reach(NZ, Z_REACH)])

    shard_v[...] = jnp.zeros_like(shard_v)
    apart = jnp.abs(lax.broadcasted_iota(jnp.int32, (16, CDW), 1) - cd_ref[col])
    one_hot = (1 - jnp.minimum(apart, 1)).astype(jnp.float32).astype(jnp.bfloat16)
    load_amp.wait()
    for p in range(ROWS):
        line = jnp.dot(one_hot, amp_v[p], preferred_element_type=jnp.float32)
        for k in range(KT):
            width = min(128, TP - 128 * k)
            shard_v[p * KT + k : p * KT + k + 1, 0:width] = line[0:1, 128 * k : 128 * k + width]
    packed = shard_v[...].astype(jnp.bfloat16)

    @pl.when(core == 0)
    def _():
        g0[y, z] = packed
        pl.semaphore_wait(barrier, NX + NZ - 1 + 2 * Y_REACH)

    @pl.when(core == 1)
    def _():
        g1[z, y] = packed
        pl.semaphore_wait(barrier, NX + NY - 1 + 2 * Z_REACH)

    def copy(src, dst, send, recv, device):
        return pltpu.make_async_remote_copy(
            src_ref=src, dst_ref=dst, send_sem=send, recv_sem=recv, device_id=device, device_id_type=MESH
        )

    def ring1(ref, n, to):
        copies = [copy(ref, ref, p1_send.at[k - 1], p1_recv.at[k - 1], to(k)) for k in range(1, n)]
        for k in sorted(range(1, n), key=lambda k: abs(k - n // 2)):
            copies[k - 1].start()
        return copies

    def ring2(buf, n, me, inner, far, to):
        def step(s, sign):
            i, hop = (me, s) if s <= far else ((me - sign * far + n) % n, s - far)
            d = 0 if sign > 0 else 1
            ref = buf.at[i]
            if s == n // 2:
                ref = ref.at[pl.ds(0 if sign > 0 else inner // 2, inner // 2)]
            return copy(ref, ref, p2_send.at[d, s - 1], p2_recv.at[d, s - 1], to(sign * hop))

        return step

    y_step = ring2(g0, NY, y, NZ, Y_REACH, along_y)
    z_step = ring2(g1, NZ, z, NY, Z_REACH, along_z)

    def block_at(half, index):
        n, me = (NY, y) if half == 0 else (NZ, z)
        return (me + distance(index) + n) % n

    def to_sibling(half, index):
        ref = (g0 if half == 0 else g1).at[block_at(half, index)]
        return copy(ref, ref, sib_send.at[index], sib_recv.at[index], sibling)

    def first(half):
        if half == 0:
            copies, step, far = ring1(g0.at[y, z], NZ, along_z), y_step, Y_REACH
        else:
            copies, step, far = ring1(g1.at[z, y], NY, along_y), z_step, Z_REACH
        for c in copies:
            c.wait_recv()
        for s in range(far, 0, -1):
            step(s, 1).start()
            step(s, -1).start()
        to_sibling(half, 0).start()
        for c in copies:
            c.wait_send()

    @pl.when(core == 0)
    def _():
        first(0)

    @pl.when(core == 1)
    def _():
        first(1)

    def arrive(half, s):
        n, step, far = (NY, y_step, Y_REACH) if half == 0 else (NZ, z_step, Z_REACH)

        @pl.when(core == half)
        def _():
            for sign in (1, -1):
                step(s, sign).wait_recv()
                if s == far:
                    for more in range(n // 2, far, -1):
                        step(more, sign).start()
                if s < n // 2:
                    to_sibling(half, 2 * s - (1 if sign > 0 else 0)).start()
            if s == n // 2:
                to_sibling(half, 2 * s - 1).start()

    device = row * NX + col
    count = counts_ref[device]
    weights = []
    for d in range(NX):
        owner = (col + d) % NX
        line = []
        for q in range(SLOTS):
            live = jnp.minimum(jnp.maximum(count - q, 0), 1)
            same = 1 - jnp.minimum(jnp.abs(target_ref[device * SLOTS + q] - owner), 1)
            line.append((live * same).astype(jnp.float32))
        weights.append(line)

    order = block_order()
    pidx[...] = jnp.full_like(pidx, -1)
    for half, index, first in order:
        if half == 0:
            for r in range(ROWS):
                step = lax.broadcasted_iota(jnp.int32, (NZ, 128), 0)
                pidx[first + NZ * r : first + NZ * r + NZ, :] = block_at(0, index) * 72 + r + 6 * step
        else:
            for r in range(ROWS):
                step = lax.broadcasted_iota(jnp.int32, (NY, 128), 0)
                pidx[first + NY * r : first + NY * r + NY, :] = block_at(1, index) * 6 + 3 + r + 72 * step
    for t in range(SLABS):
        lanes = lax.broadcasted_iota(jnp.int32, (SLAB * SLABS, 128), 1) + 128 * t
        perm[:, 128 * t : 128 * t + 128] = jnp.where(pidx[...] == lanes, 1.0, 0.0).astype(jnp.bfloat16)
    a_f[:, PAIRS:, :] = jnp.zeros((KT, SLAB * SLABS - PAIRS, 128), jnp.float32)

    def unpack(half, index, first):
        n = NZ if half == 0 else NY
        i = block_at(half, index)

        @pl.when(core != half)
        def _():
            to_sibling(half, index).wait_recv()

        block = (g0 if half == 0 else g1)[i]
        wide[0 : n * 64, :] = block.reshape(n * 64, 128).astype(jnp.float32)

        @pl.loop(0, KT)
        def _(k):
            for r in range(ROWS):
                a_f[k, first + n * r : first + n * r + n, :] = wide[pl.ds(r * KT + k, n, stride=64), :]

    def x_copy(j, d):
        return copy(p_send.at[d - 1, j], p_got.at[d - 1, j], x_send.at[j, d - 1], x_recv.at[j, d - 1], along_x(d))

    def encode(part):
        top = jnp.maximum(jnp.max(jnp.abs(part), axis=0, keepdims=True), 2.0**-110)
        e = jnp.ceil(jnp.log2(top) * 64.0)
        codes = jnp.round(part * (jnp.exp2(e * (-1 / 64)) * LEVELS)).astype(jnp.int32)
        scale = jnp.broadcast_to(e.astype(jnp.int32), (CODED - RB, SLAB))
        return jnp.concatenate([codes, scale], axis=0).astype(jnp.int16)

    def decode(coded):
        wide = coded.astype(jnp.int32)
        scale = jnp.exp2(wide[RB : RB + 1].astype(jnp.float32) * (1 / 64)) * (1 / LEVELS)
        return wide[0:RB].astype(jnp.float32) * scale

    def slab(j):
        for k in range(KT):
            a_b[:, 128 * k : 128 * k + 128] = a_f[k, SLAB * j : SLAB * j + SLAB, :].astype(jnp.bfloat16)
        terms = [
            lax.dot_general(int_v[q], a_b[:, 0:TP], NT, preferred_element_type=jnp.float32) for q in range(SLOTS)
        ]

        def part(d):
            return sum(w * t for w, t in zip(weights[d], terms))

        for d in (2, 1, 3):
            p_send[d - 1, j] = encode(part(d))
            x_copy(j, d).start()
        p_own[j] = part(0)

    def finish(j):
        whole = p_own[j]
        for d in (1, 3, 2):
            x_copy(j, d).wait_recv()
            whole = whole + decode(p_got[d - 1, j])
        high = whole.astype(jnp.bfloat16)
        low = (whole - high.astype(jnp.float32)).astype(jnp.bfloat16)
        mine = perm[SLAB * j : SLAB * j + SLAB, 0:PAIRS]
        more = jnp.dot(high, mine, preferred_element_type=jnp.float32)
        more = more + jnp.dot(low, mine, preferred_element_type=jnp.float32)
        if j == 0:
            out_ref[...] = more
        else:
            out_ref[...] = out_ref[...] + more

    at_row = {(h, i): f for h, i, f in order}

    def take(*blocks):
        for b in blocks:
            unpack(*b, at_row[b])

    take((1, 0), (0, 0))
    arrive(1, 3)
    arrive(0, 2)
    arrive(1, 2)
    arrive(0, 1)
    arrive(1, 1)
    take((1, 1), (1, 2), (1, 3), (1, 4))
    load_int.wait()
    slab(0)
    take((0, 1), (0, 2))
    take((1, 5), (1, 6))
    slab(1)
    arrive(1, 4)
    arrive(0, 3)
    take((0, 3), (0, 4))
    take((1, 7), (1, 8))
    slab(2)
    arrive(1, 5)
    arrive(1, 6)
    arrive(0, 4)
    take((0, 5), (0, 6))
    take((1, 9), (1, 10))
    slab(3)
    take((1, 11), (0, 7))
    slab(4)
    for j in range(SLABS):
        finish(j)

    @pl.when(core == 0)
    def _():
        for s in range(1, NY // 2 + 1):
            y_step(s, 1).wait_send()
            y_step(s, -1).wait_send()
        for index in range(NY):
            to_sibling(0, index).wait_send()

    @pl.when(core == 1)
    def _():
        for s in range(1, NZ // 2 + 1):
            z_step(s, 1).wait_send()
            z_step(s, -1).wait_send()
        for index in range(NZ):
            to_sibling(1, index).wait_send()

    for j in range(SLABS):
        for d in range(1, NX):
            x_copy(j, d).wait_send()


def local(amplitudes, integrals, cd_tile, target, counts):
    amp = jnp.transpose(amplitudes, (1, 0, 2))
    anywhere, scalars = pl.BlockSpec(memory_space=pl.ANY), pl.BlockSpec(memory_space=pltpu.SMEM)
    dma = pltpu.SemaphoreType.DMA
    residual = pl.pallas_call(
        kernel,
        out_shape=jax.ShapeDtypeStruct((RB, PAIRS), jnp.float32),
        in_specs=[scalars, scalars, scalars, anywhere, anywhere],
        out_specs=pl.BlockSpec(memory_space=pltpu.VMEM),
        scratch_shapes=[
            pltpu.VMEM(amp.shape, jnp.bfloat16),
            pltpu.VMEM(integrals.shape, jnp.bfloat16),
            pltpu.VMEM((64, 128), jnp.float32),
            pltpu.VMEM((NY, NZ, 64, 128), jnp.bfloat16),
            pltpu.VMEM((NZ, NY, 64, 128), jnp.bfloat16),
            pltpu.VMEM((NZ * 64, 128), jnp.float32),
            pltpu.VMEM((KT, SLAB * SLABS, 128), jnp.float32),
            pltpu.VMEM((SLAB, KT * 128), jnp.bfloat16),
            pltpu.VMEM((SLAB * SLABS, SLAB * SLABS), jnp.bfloat16),
            pltpu.VMEM((SLAB * SLABS, 128), jnp.int32),
            pltpu.VMEM((SLABS, RB, SLAB), jnp.float32),
            pltpu.VMEM((3, SLABS, CODED, SLAB), jnp.int16),
            pltpu.VMEM((3, SLABS, CODED, SLAB), jnp.int16),
            dma((2,)),
            dma((11,)),
            dma((11,)),
            dma((2, 6)),
            dma((2, 6)),
            dma((12,)),
            dma((12,)),
            dma((SLABS, 3)),
            dma((SLABS, 3)),
        ],
        compiler_params=pltpu.CompilerParams(
            collective_id=0, has_side_effects=True, vmem_limit_bytes=56 * 1024 * 1024
        ),
        cost_estimate=pl.CostEstimate(flops=2 * SLOTS * RB * PAIRS * TP, bytes_accessed=6 * 10**6, transcendentals=0),
    )(cd_tile, target, counts, amp, integrals)
    return jnp.transpose(residual)[None]


def solution(mesh):
    in_specs = (P(None, "row", None), P(("row", "col"), None, None), P(), P(), P())
    out_specs = P(("row", "col"), None, None)
    return jax.shard_map(local, mesh=mesh, in_specs=in_specs, out_specs=out_specs, check_vma=False)
```

```python
import jax
import jax.numpy as jnp
from jax import lax
from jax.experimental import pallas as pl
from jax.experimental.pallas import tpu as pltpu
from jax.sharding import PartitionSpec as P

MESH = pl.DeviceIdType.MESH
NY, NZ, NX = 8, 12, 4
ROWS = 3
KT = 20
TP = 2500
CDW = 96
PAIRS = 576
RB = 200
SLOTS = 4
Y_REACH, Z_REACH = 2, 3
Z_NEAR, Y_NEAR = 7, 5
SLAB = 128
SLABS = 5
CODED = 208
FOLD, FOLDED = 104, 112
LEVELS = 32000.0
NT = (((1,), (1,)), ((), ()))


def block_order():
    order = []
    row = 0
    for half, index in (
        [(1, 0), (0, 0), (1, 1), (1, 2), (1, 3), (1, 4), (0, 1), (0, 2), (1, 5), (1, 6), (0, 3), (0, 4)]
        + [(1, 7), (1, 8), (0, 5), (0, 6), (1, 9), (1, 10), (1, 11), (0, 7)]
    ):
        order.append((half, index, row))
        row += 36 if half == 0 else 24
    return order


def slot_of(k, n):
    return 0 if k == 0 else 2 * k - 1 if k <= n // 2 else 2 * (n - k)


def distance(index):
    return -((index + 1) // 2) if index % 2 else index // 2


def kernel(
    cd_hbm, target_hbm, counts_hbm, amp_hbm, int_hbm, out_ref,
    cd_ref, target_ref, counts_ref, amp_v, int_v, shard_v, g0, g1, wide, a_f, a_b, perm, pidx,
    p_own, p_send, p_got,
    load_sem, p1_send, p1_recv, p2_send, p2_recv, sib_send, sib_recv, x_send, x_recv,
):
    row, col = lax.axis_index("row"), lax.axis_index("col")
    y, z, core = row // (2 * NZ), (row // 2) % NZ, row % 2

    def at(yy, zz, cc):
        return ((yy * NZ + zz) * 2 + cc, col)

    def along_y(k):
        return at((y + k + NY) % NY, z, core)

    def along_z(k):
        return at(y, (z + k + NZ) % NZ, core)

    sibling = at(y, z, 1 - core)
    def along_x(k):
        return (row, (col + k) % NX)


    load_amp = pltpu.make_async_copy(amp_hbm, amp_v, load_sem.at[0])
    load_int = pltpu.make_async_copy(int_hbm, int_v, load_sem.at[1])
    load_cd = pltpu.make_async_copy(cd_hbm, cd_ref, load_sem.at[2])
    load_target = pltpu.make_async_copy(target_hbm, target_ref, load_sem.at[3])
    load_counts = pltpu.make_async_copy(counts_hbm, counts_ref, load_sem.at[4])
    load_cd.start()
    load_amp.start()
    load_target.start()
    load_counts.start()

    barrier = pltpu.get_barrier_semaphore()

    def greet(others):
        for other in others:
            pl.semaphore_signal(barrier, inc=1, device_id=other, device_id_type=MESH)

    def reach(n, r):
        return [k for s in range(r, 0, -1) for k in (s, -s)]

    greet([sibling] + [along_x(k) for k in range(1, NX)])

    @pl.when(core == 0)
    def _():
        greet([along_z(k) for k in range(1, NZ)] + [along_y(k) for k in reach(NY, Y_REACH)])

    @pl.when(core == 1)
    def _():
        greet([along_y(k) for k in range(1, NY)] + [along_z(k) for k in reach(NZ, Z_REACH)])

    shard_v[...] = jnp.zeros_like(shard_v)
    load_cd.wait()
    apart = jnp.abs(lax.broadcasted_iota(jnp.int32, (16, CDW), 1) - cd_ref[col])
    one_hot = (1 - jnp.minimum(apart, 1)).astype(jnp.float32).astype(jnp.bfloat16)
    load_amp.wait()
    load_int.start()
    for p in range(ROWS):
        line = jnp.dot(one_hot, amp_v[p], preferred_element_type=jnp.float32)
        for k in range(KT):
            width = min(128, TP - 128 * k)
            shard_v[p * KT + k : p * KT + k + 1, 0:width] = line[0:1, 128 * k : 128 * k + width]
    packed = shard_v[...].astype(jnp.bfloat16)

    @pl.when(core == 0)
    def _():
        g0[y, 0] = packed
        pl.semaphore_wait(barrier, NX + NZ - 1 + 2 * Y_REACH)

    @pl.when(core == 1)
    def _():
        g1[z, 0] = packed
        pl.semaphore_wait(barrier, NX + NY - 1 + 2 * Z_REACH)

    def copy(src, dst, send, recv, device):
        return pltpu.make_async_remote_copy(
            src_ref=src, dst_ref=dst, send_sem=send, recv_sem=recv, device_id=device, device_id_type=MESH
        )

    def ring1(block, n, to):
        own, copies = block.at[0], {}
        for k in sorted(range(1, n), key=lambda k: min(k, n - k)):
            place = block.at[slot_of(n - k, n)]
            copies[k] = copy(own, place, p1_send.at[k - 1], p1_recv.at[k - 1], to(k))
            copies[k].start()
        return copies

    def ring2(buf, n, me, inner, near, far, to):
        def step(s, sign, piece):
            i, hop = (me, s) if s <= far else ((me - sign * far + n) % n, s - far)
            d = 0 if sign > 0 else 1
            ref = buf.at[i, pl.ds(0, near) if piece == 0 else pl.ds(near, inner - near)]
            return copy(ref, ref, p2_send.at[d, s - 1, piece], p2_recv.at[d, s - 1, piece], to(sign * hop))

        return step

    def pieces(n, s, sign):
        return (0, 1) if s < n // 2 else (0,) if sign > 0 else (1,)

    y_step = ring2(g0, NY, y, NZ, Z_NEAR, Y_REACH, along_y)
    z_step = ring2(g1, NZ, z, NY, Y_NEAR, Z_REACH, along_z)

    def block_at(half, index):
        n, me = (NY, y) if half == 0 else (NZ, z)
        return (me + distance(index) + n) % n

    def to_sibling(half, index):
        ref = (g0 if half == 0 else g1).at[block_at(half, index)]
        return copy(ref, ref, sib_send.at[index], sib_recv.at[index], sibling)

    def first(half):
        if half == 0:
            block, inner, to, step, n, far, near = g0.at[y], NZ, along_z, y_step, NY, Y_REACH, Z_NEAR
        else:
            block, inner, to, step, n, far, near = g1.at[z], NY, along_y, z_step, NZ, Z_REACH, Y_NEAR
        copies = ring1(block, inner, to)
        for piece in (0, 1):
            for k in range(1, inner):
                if (slot_of(inner - k, inner) < near) == (piece == 0):
                    copies[k].wait_recv()
            for s in range(far, 0, -1):
                for sign in (1, -1):
                    step(s, sign, piece).start()
        to_sibling(half, 0).start()
        for c in copies.values():
            c.wait_send()

    @pl.when(core == 0)
    def _():
        first(0)

    @pl.when(core == 1)
    def _():
        first(1)

    def second(half):
        n, step, far = (NY, y_step, Y_REACH) if half == 0 else (NZ, z_step, Z_REACH)
        for piece in (0, 1):
            for sign in (1, -1):
                step(far, sign, piece).wait_recv()
                for more in range(n // 2, far, -1):
                    if piece in pieces(n, more, sign):
                        step(more, sign, piece).start()
        for sign in (1, -1):
            to_sibling(half, 2 * far - (1 if sign > 0 else 0)).start()

    def arrive(half, s):
        n, step = (NY, y_step) if half == 0 else (NZ, z_step)

        @pl.when(core == half)
        def _():
            for sign in (1, -1):
                for piece in pieces(n, s, sign):
                    step(s, sign, piece).wait_recv()
                if s < n // 2:
                    to_sibling(half, 2 * s - (1 if sign > 0 else 0)).start()
            if s == n // 2:
                to_sibling(half, 2 * s - 1).start()

    load_target.wait()
    load_counts.wait()
    device = row * NX + col
    count = counts_ref[device]
    weights = []
    for d in range(NX):
        owner = (col + d) % NX
        line = []
        for q in range(SLOTS):
            live = jnp.minimum(jnp.maximum(count - q, 0), 1)
            same = 1 - jnp.minimum(jnp.abs(target_ref[device * SLOTS + q] - owner), 1)
            line.append((live * same).astype(jnp.float32))
        weights.append(line)

    order = block_order()
    pidx[...] = jnp.full_like(pidx, -1)
    for half, index, first_row in order:
        n, me = (NZ, z) if half == 0 else (NY, y)
        place = lax.broadcasted_iota(jnp.int32, (n, 128), 0)
        away = (place + 1) // 2
        source = me + jnp.where(place % 2 == 1, away, -away)
        source = jnp.where(source < 0, source + n, jnp.where(source >= n, source - n, source))
        for r in range(ROWS):
            if half == 0:
                pair = block_at(0, index) * 72 + source * 6 + r
            else:
                pair = source * 72 + block_at(1, index) * 6 + 3 + r
            pidx[first_row + n * r : first_row + n * r + n, :] = pair
    for t in range(SLABS):
        lanes = lax.broadcasted_iota(jnp.int32, (SLAB * SLABS, 128), 1) + 128 * t
        perm[:, 128 * t : 128 * t + 128] = jnp.where(pidx[...] == lanes, 1.0, 0.0).astype(jnp.bfloat16)
    a_f[:, PAIRS:, :] = jnp.zeros((KT, SLAB * SLABS - PAIRS, 128), jnp.float32)

    def unpack(half, index, first):
        n = NZ if half == 0 else NY
        i = block_at(half, index)

        @pl.when(core != half)
        def _():
            to_sibling(half, index).wait_recv()

        block = (g0 if half == 0 else g1)[i]
        wide[0 : n * 64, :] = block.reshape(n * 64, 128).astype(jnp.float32)

        @pl.loop(0, KT)
        def _(k):
            for r in range(ROWS):
                a_f[k, first + n * r : first + n * r + n, :] = wide[pl.ds(r * KT + k, n, stride=64), :]

    def x_copy(j, d):
        rows = pl.ds(0, CODED if j < SLABS - 1 else FOLDED)
        src, dst = p_send.at[d - 1, j, rows], p_got.at[d - 1, j, rows]
        return copy(src, dst, x_send.at[j, d - 1], x_recv.at[j, d - 1], along_x(d))

    def encode(part, j):
        top = jnp.maximum(jnp.max(jnp.abs(part), axis=0, keepdims=True), 2.0**-110)
        e = jnp.ceil(jnp.log2(top) * 64.0)
        codes = jnp.round(part * (jnp.exp2(e * (-1 / 64)) * LEVELS)).astype(jnp.int32)
        scale = jnp.broadcast_to(e.astype(jnp.int32), (CODED - RB, SLAB))
        if j == SLABS - 1:
            lower = pltpu.roll(codes[FOLD:], 64, 1)
            lower = jnp.concatenate([lower, jnp.zeros((2 * FOLD - RB, SLAB), jnp.int32)], axis=0)
            codes = codes[0:FOLD] + lower
        return jnp.concatenate([codes, scale], axis=0).astype(jnp.int16)

    def decode(d, j):
        if j < SLABS - 1:
            wide = p_got[d - 1, j].astype(jnp.int32)
            codes, e = wide[0:RB], wide[RB : RB + 1]
        else:
            wide = p_got[d - 1, j, 0:FOLDED].astype(jnp.int32)
            codes = jnp.concatenate([wide[0:FOLD], pltpu.roll(wide[0 : RB - FOLD], 64, 1)], axis=0)
            e = wide[FOLD : FOLD + 1]
        return codes.astype(jnp.float32) * (jnp.exp2(e.astype(jnp.float32) * (1 / 64)) * (1 / LEVELS))

    def slab(j):
        for k in range(KT):
            a_b[:, 128 * k : 128 * k + 128] = a_f[k, SLAB * j : SLAB * j + SLAB, :].astype(jnp.bfloat16)
        terms = [
            lax.dot_general(int_v[q], a_b[:, 0:TP], NT, preferred_element_type=jnp.float32) for q in range(SLOTS)
        ]

        def part(d):
            return sum(w * t for w, t in zip(weights[d], terms))

        for d in (2, 1, 3):
            coded = encode(part(d), j)
            p_send[d - 1, j, 0 : coded.shape[0]] = coded
            x_copy(j, d).start()
        p_own[j] = part(0)

    def finish(j):
        whole = p_own[j]
        for d in (1, 3, 2):
            x_copy(j, d).wait_recv()
            whole = whole + decode(d, j)
        high = whole.astype(jnp.bfloat16)
        low = (whole - high.astype(jnp.float32)).astype(jnp.bfloat16)
        mine = perm[SLAB * j : SLAB * j + SLAB, 0:PAIRS]
        more = jnp.dot(high, mine, preferred_element_type=jnp.float32)
        more = more + jnp.dot(low, mine, preferred_element_type=jnp.float32)
        if j == 0:
            out_ref[...] = more
        else:
            out_ref[...] = out_ref[...] + more

    at_row = {(h, i): f for h, i, f in order}

    def take(*blocks):
        for b in blocks:
            unpack(*b, at_row[b])

    @pl.when(core == 0)
    def _():
        second(0)

    @pl.when(core == 1)
    def _():
        second(1)

    take((1, 0), (0, 0))
    arrive(1, 2)
    arrive(0, 1)
    arrive(1, 1)
    take((1, 1), (1, 2), (1, 3), (1, 4))
    load_int.wait()
    slab(0)
    take((0, 1), (0, 2))
    take((1, 5), (1, 6))
    slab(1)
    arrive(1, 4)
    arrive(0, 3)
    take((0, 3), (0, 4))
    take((1, 7), (1, 8))
    slab(2)
    arrive(1, 5)
    arrive(1, 6)
    finish(0)
    arrive(0, 4)
    take((0, 5), (0, 6))
    take((1, 9), (1, 10))
    slab(3)
    take((1, 11), (0, 7))
    slab(4)
    for j in range(1, SLABS):
        finish(j)

    def sent(n, step):
        for s in range(1, n // 2 + 1):
            for sign in (1, -1):
                for piece in pieces(n, s, sign):
                    step(s, sign, piece).wait_send()

    @pl.when(core == 0)
    def _():
        sent(NY, y_step)
        for index in range(NY):
            to_sibling(0, index).wait_send()

    @pl.when(core == 1)
    def _():
        sent(NZ, z_step)
        for index in range(NZ):
            to_sibling(1, index).wait_send()

    for j in range(SLABS):
        for d in range(1, NX):
            x_copy(j, d).wait_send()


def local(amplitudes, integrals, cd_tile, target, counts):
    amp = jnp.transpose(amplitudes, (1, 0, 2))
    anywhere = pl.BlockSpec(memory_space=pl.ANY)
    dma = pltpu.SemaphoreType.DMA
    residual = pl.pallas_call(
        kernel,
        out_shape=jax.ShapeDtypeStruct((RB, PAIRS), jnp.float32),
        in_specs=[anywhere] * 5,
        out_specs=pl.BlockSpec(memory_space=pltpu.VMEM),
        scratch_shapes=[
            pltpu.SMEM(cd_tile.shape, jnp.int32),
            pltpu.SMEM(target.shape, jnp.int32),
            pltpu.SMEM(counts.shape, jnp.int32),
            pltpu.VMEM(amp.shape, jnp.bfloat16),
            pltpu.VMEM(integrals.shape, jnp.bfloat16),
            pltpu.VMEM((64, 128), jnp.float32),
            pltpu.VMEM((NY, NZ, 64, 128), jnp.bfloat16),
            pltpu.VMEM((NZ, NY, 64, 128), jnp.bfloat16),
            pltpu.VMEM((NZ * 64, 128), jnp.float32),
            pltpu.VMEM((KT, SLAB * SLABS, 128), jnp.float32),
            pltpu.VMEM((SLAB, KT * 128), jnp.bfloat16),
            pltpu.VMEM((SLAB * SLABS, SLAB * SLABS), jnp.bfloat16),
            pltpu.VMEM((SLAB * SLABS, 128), jnp.int32),
            pltpu.VMEM((SLABS, RB, SLAB), jnp.float32),
            pltpu.VMEM((3, SLABS, CODED, SLAB), jnp.int16),
            pltpu.VMEM((3, SLABS, CODED, SLAB), jnp.int16),
            dma((5,)),
            dma((11,)),
            dma((11,)),
            dma((2, 6, 2)),
            dma((2, 6, 2)),
            dma((12,)),
            dma((12,)),
            dma((SLABS, 3)),
            dma((SLABS, 3)),
        ],
        compiler_params=pltpu.CompilerParams(
            collective_id=0, has_side_effects=True, vmem_limit_bytes=56 * 1024 * 1024
        ),
        cost_estimate=pl.CostEstimate(flops=2 * SLOTS * RB * PAIRS * TP, bytes_accessed=6 * 10**6, transcendentals=0),
    )(cd_tile, target, counts, amp, integrals)
    return jnp.transpose(residual)[None]


def solution(mesh):
    in_specs = (P(None, "row", None), P(("row", "col"), None, None), P(), P(), P())
    out_specs = P(("row", "col"), None, None)
    return jax.shard_map(local, mesh=mesh, in_specs=in_specs, out_specs=out_specs, check_vma=False)
```

```python
import jax
import jax.numpy as jnp
from jax import lax
from jax.experimental import pallas as pl
from jax.experimental.pallas import tpu as pltpu
from jax.sharding import PartitionSpec as P

MESH = pl.DeviceIdType.MESH
NY, NZ, NX = 8, 12, 4
ROWS = 3
KT = 20
TP = 2500
CDW = 96
PAIRS = 576
RB = 200
SLOTS = 4
Y_REACH, Z_REACH = 2, 3
Z_NEAR, Y_NEAR = 5, 3
SLAB = 128
SLABS = 5
CODED = 208
FOLD, FOLDED = 104, 112
LEVELS = 32000.0
NT = (((1,), (1,)), ((), ()))


def block_order():
    order = []
    row = 0
    for half, index in (
        [(1, 0), (0, 0), (1, 1), (1, 2), (1, 3), (1, 4), (0, 1), (0, 2), (1, 5), (1, 6), (0, 3), (0, 4)]
        + [(1, 7), (1, 8), (0, 5), (0, 6), (1, 9), (1, 10), (1, 11), (0, 7)]
    ):
        order.append((half, index, row))
        row += 36 if half == 0 else 24
    return order


def slot_of(k, n):
    return 0 if k == 0 else 2 * k - 1 if k <= n // 2 else 2 * (n - k)


def distance(index):
    return -((index + 1) // 2) if index % 2 else index // 2


def kernel(
    cd_hbm, target_hbm, counts_hbm, amp_hbm, int_hbm, out_ref,
    cd_ref, target_ref, counts_ref, amp_v, int_v, shard_v, g0, g1, wide, a_f, a_b, perm, pidx,
    p_own, p_send, p_got,
    load_sem, p1_send, p1_recv, p2_send, p2_recv, sib_send, sib_recv, x_send, x_recv,
):
    row, col = lax.axis_index("row"), lax.axis_index("col")
    y, z, core = row // (2 * NZ), (row // 2) % NZ, row % 2

    def at(yy, zz, cc):
        return ((yy * NZ + zz) * 2 + cc, col)

    def along_y(k):
        return at((y + k + NY) % NY, z, core)

    def along_z(k):
        return at(y, (z + k + NZ) % NZ, core)

    sibling = at(y, z, 1 - core)
    def along_x(k):
        return (row, (col + k) % NX)


    load_amp = pltpu.make_async_copy(amp_hbm, amp_v, load_sem.at[0])
    load_int = pltpu.make_async_copy(int_hbm, int_v, load_sem.at[1])
    load_cd = pltpu.make_async_copy(cd_hbm, cd_ref, load_sem.at[2])
    load_target = pltpu.make_async_copy(target_hbm, target_ref, load_sem.at[3])
    load_counts = pltpu.make_async_copy(counts_hbm, counts_ref, load_sem.at[4])
    load_cd.start()
    load_amp.start()
    load_target.start()
    load_counts.start()

    barrier = pltpu.get_barrier_semaphore()

    def greet(others):
        for other in others:
            pl.semaphore_signal(barrier, inc=1, device_id=other, device_id_type=MESH)

    def reach(n, r):
        return [k for s in range(r, 0, -1) for k in (s, -s)]

    greet([sibling] + [along_x(k) for k in range(1, NX)])

    @pl.when(core == 0)
    def _():
        greet([along_z(k) for k in range(1, NZ)] + [along_y(k) for k in reach(NY, Y_REACH)])

    @pl.when(core == 1)
    def _():
        greet([along_y(k) for k in range(1, NY)] + [along_z(k) for k in reach(NZ, Z_REACH)])

    shard_v[...] = jnp.zeros_like(shard_v)
    load_cd.wait()
    apart = jnp.abs(lax.broadcasted_iota(jnp.int32, (16, CDW), 1) - cd_ref[col])
    one_hot = (1 - jnp.minimum(apart, 1)).astype(jnp.float32).astype(jnp.bfloat16)
    load_amp.wait()
    load_int.start()
    for p in range(ROWS):
        line = jnp.dot(one_hot, amp_v[p], preferred_element_type=jnp.float32)
        for k in range(KT):
            width = min(128, TP - 128 * k)
            shard_v[p * KT + k : p * KT + k + 1, 0:width] = line[0:1, 128 * k : 128 * k + width]
    packed = shard_v[...].astype(jnp.bfloat16)

    @pl.when(core == 0)
    def _():
        g0[y, 0] = packed
        pl.semaphore_wait(barrier, NX + NZ - 1 + 2 * Y_REACH)

    @pl.when(core == 1)
    def _():
        g1[z, 0] = packed
        pl.semaphore_wait(barrier, NX + NY - 1 + 2 * Z_REACH)

    def copy(src, dst, send, recv, device):
        return pltpu.make_async_remote_copy(
            src_ref=src, dst_ref=dst, send_sem=send, recv_sem=recv, device_id=device, device_id_type=MESH
        )

    def ring1(block, n, to):
        own, copies = block.at[0], {}
        for k in sorted(range(1, n), key=lambda k: min(k, n - k)):
            place = block.at[slot_of(n - k, n)]
            copies[k] = copy(own, place, p1_send.at[k - 1], p1_recv.at[k - 1], to(k))
            copies[k].start()
        return copies

    def ring2(buf, n, me, inner, near, far, to):
        def step(s, sign, piece):
            i, hop = (me, s) if s <= far else ((me - sign * far + n) % n, s - far)
            d = 0 if sign > 0 else 1
            ref = buf.at[i, pl.ds(0, near) if piece == 0 else pl.ds(near, inner - near)]
            return copy(ref, ref, p2_send.at[d, s - 1, piece], p2_recv.at[d, s - 1, piece], to(sign * hop))

        return step

    def pieces(n, s, sign):
        return (0, 1) if s < n // 2 else (0,) if sign > 0 else (1,)

    y_step = ring2(g0, NY, y, NZ, Z_NEAR, Y_REACH, along_y)
    z_step = ring2(g1, NZ, z, NY, Y_NEAR, Z_REACH, along_z)

    def block_at(half, index):
        n, me = (NY, y) if half == 0 else (NZ, z)
        return (me + distance(index) + n) % n

    def to_sibling(half, index):
        ref = (g0 if half == 0 else g1).at[block_at(half, index)]
        return copy(ref, ref, sib_send.at[index], sib_recv.at[index], sibling)

    def first(half):
        if half == 0:
            block, inner, to, step, n, far, near = g0.at[y], NZ, along_z, y_step, NY, Y_REACH, Z_NEAR
        else:
            block, inner, to, step, n, far, near = g1.at[z], NY, along_y, z_step, NZ, Z_REACH, Y_NEAR
        copies = ring1(block, inner, to)
        for piece in (0, 1):
            for k in range(1, inner):
                if (slot_of(inner - k, inner) < near) == (piece == 0):
                    copies[k].wait_recv()
            for s in range(far, 0, -1):
                for sign in (1, -1):
                    step(s, sign, piece).start()
        to_sibling(half, 0).start()
        for c in copies.values():
            c.wait_send()

    @pl.when(core == 0)
    def _():
        first(0)

    @pl.when(core == 1)
    def _():
        first(1)

    def second(half):
        n, step, far = (NY, y_step, Y_REACH) if half == 0 else (NZ, z_step, Z_REACH)
        for piece in (0, 1):
            for sign in (1, -1):
                step(far, sign, piece).wait_recv()
                for more in range(n // 2, far, -1):
                    if piece in pieces(n, more, sign):
                        step(more, sign, piece).start()
        for sign in (1, -1):
            to_sibling(half, 2 * far - (1 if sign > 0 else 0)).start()

    def arrive(half, s):
        n, step = (NY, y_step) if half == 0 else (NZ, z_step)

        @pl.when(core == half)
        def _():
            for sign in (1, -1):
                for piece in pieces(n, s, sign):
                    step(s, sign, piece).wait_recv()
                if s < n // 2:
                    to_sibling(half, 2 * s - (1 if sign > 0 else 0)).start()
            if s == n // 2:
                to_sibling(half, 2 * s - 1).start()

    load_target.wait()
    load_counts.wait()
    device = row * NX + col
    count = counts_ref[device]
    weights = []
    for d in range(NX):
        owner = (col + d) % NX
        line = []
        for q in range(SLOTS):
            live = jnp.minimum(jnp.maximum(count - q, 0), 1)
            same = 1 - jnp.minimum(jnp.abs(target_ref[device * SLOTS + q] - owner), 1)
            line.append((live * same).astype(jnp.float32))
        weights.append(line)

    order = block_order()
    pidx[...] = jnp.full_like(pidx, -1)
    for half, index, first_row in order:
        n, me = (NZ, z) if half == 0 else (NY, y)
        place = lax.broadcasted_iota(jnp.int32, (n, 128), 0)
        away = (place + 1) // 2
        source = me + jnp.where(place % 2 == 1, away, -away)
        source = jnp.where(source < 0, source + n, jnp.where(source >= n, source - n, source))
        for r in range(ROWS):
            if half == 0:
                pair = block_at(0, index) * 72 + source * 6 + r
            else:
                pair = source * 72 + block_at(1, index) * 6 + 3 + r
            pidx[first_row + n * r : first_row + n * r + n, :] = pair
    for t in range(SLABS):
        lanes = lax.broadcasted_iota(jnp.int32, (SLAB * SLABS, 128), 1) + 128 * t
        perm[:, 128 * t : 128 * t + 128] = jnp.where(pidx[...] == lanes, 1.0, 0.0).astype(jnp.bfloat16)
    a_f[:, PAIRS:, :] = jnp.zeros((KT, SLAB * SLABS - PAIRS, 128), jnp.float32)

    def unpack(half, index, first):
        n = NZ if half == 0 else NY
        i = block_at(half, index)

        @pl.when(core != half)
        def _():
            to_sibling(half, index).wait_recv()

        block = (g0 if half == 0 else g1)[i]
        wide[0 : n * 64, :] = block.reshape(n * 64, 128).astype(jnp.float32)

        @pl.loop(0, KT, unroll=5)
        def _(k):
            for r in range(ROWS):
                a_f[k, first + n * r : first + n * r + n, :] = wide[pl.ds(r * KT + k, n, stride=64), :]

    def x_copy(j, d):
        rows = pl.ds(0, CODED if j < SLABS - 1 else FOLDED)
        src, dst = p_send.at[d - 1, j, rows], p_got.at[d - 1, j, rows]
        return copy(src, dst, x_send.at[j, d - 1], x_recv.at[j, d - 1], along_x(d))

    def encode(part, j):
        top = jnp.maximum(jnp.max(jnp.abs(part), axis=0, keepdims=True), 2.0**-110)
        e = jnp.ceil(jnp.log2(top) * 64.0)
        codes = jnp.round(part * (jnp.exp2(e * (-1 / 64)) * LEVELS)).astype(jnp.int32)
        scale = jnp.broadcast_to(e.astype(jnp.int32), (CODED - RB, SLAB))
        if j == SLABS - 1:
            lower = pltpu.roll(codes[FOLD:], 64, 1)
            lower = jnp.concatenate([lower, jnp.zeros((2 * FOLD - RB, SLAB), jnp.int32)], axis=0)
            codes = codes[0:FOLD] + lower
        return jnp.concatenate([codes, scale], axis=0).astype(jnp.int16)

    def decode(d, j):
        if j < SLABS - 1:
            wide = p_got[d - 1, j].astype(jnp.int32)
            codes, e = wide[0:RB], wide[RB : RB + 1]
        else:
            wide = p_got[d - 1, j, 0:FOLDED].astype(jnp.int32)
            codes = jnp.concatenate([wide[0:FOLD], pltpu.roll(wide[0 : RB - FOLD], 64, 1)], axis=0)
            e = wide[FOLD : FOLD + 1]
        return codes.astype(jnp.float32) * (jnp.exp2(e.astype(jnp.float32) * (1 / 64)) * (1 / LEVELS))

    def slab(j):
        for k in range(KT):
            a_b[:, 128 * k : 128 * k + 128] = a_f[k, SLAB * j : SLAB * j + SLAB, :].astype(jnp.bfloat16)
        terms = [
            lax.dot_general(int_v[q], a_b[:, 0:TP], NT, preferred_element_type=jnp.float32) for q in range(SLOTS)
        ]

        def part(d):
            return sum(w * t for w, t in zip(weights[d], terms))

        for d in (2, 1, 3):
            coded = encode(part(d), j)
            p_send[d - 1, j, 0 : coded.shape[0]] = coded
            x_copy(j, d).start()
        p_own[j] = part(0)

    def finish(j):
        whole = p_own[j]
        for d in (1, 3, 2):
            x_copy(j, d).wait_recv()
            whole = whole + decode(d, j)
        high = whole.astype(jnp.bfloat16)
        low = (whole - high.astype(jnp.float32)).astype(jnp.bfloat16)
        mine = perm[SLAB * j : SLAB * j + SLAB, 0:PAIRS]
        more = jnp.dot(high, mine, preferred_element_type=jnp.float32)
        more = more + jnp.dot(low, mine, preferred_element_type=jnp.float32)
        if j == 0:
            out_ref[...] = more
        else:
            out_ref[...] = out_ref[...] + more

    at_row = {(h, i): f for h, i, f in order}

    def take(*blocks):
        for b in blocks:
            unpack(*b, at_row[b])

    @pl.when(core == 0)
    def _():
        second(0)

    @pl.when(core == 1)
    def _():
        second(1)

    take((1, 0), (0, 0))
    arrive(1, 2)
    arrive(0, 1)
    arrive(1, 1)
    take((1, 1), (1, 2), (1, 3), (1, 4))
    load_int.wait()
    slab(0)
    take((0, 1), (0, 2))
    take((1, 5), (1, 6))
    slab(1)
    arrive(1, 4)
    arrive(0, 3)
    take((0, 3), (0, 4))
    take((1, 7), (1, 8))
    slab(2)
    arrive(1, 5)
    arrive(1, 6)
    arrive(0, 4)
    take((0, 5), (0, 6))
    take((1, 9), (1, 10))
    slab(3)
    take((1, 11), (0, 7))
    slab(4)
    for j in range(SLABS):
        finish(j)

    def sent(n, step):
        for s in range(1, n // 2 + 1):
            for sign in (1, -1):
                for piece in pieces(n, s, sign):
                    step(s, sign, piece).wait_send()

    @pl.when(core == 0)
    def _():
        sent(NY, y_step)
        for index in range(NY):
            to_sibling(0, index).wait_send()

    @pl.when(core == 1)
    def _():
        sent(NZ, z_step)
        for index in range(NZ):
            to_sibling(1, index).wait_send()

    for j in range(SLABS):
        for d in range(1, NX):
            x_copy(j, d).wait_send()


def local(amplitudes, integrals, cd_tile, target, counts):
    amp = jnp.transpose(amplitudes, (1, 0, 2))
    anywhere = pl.BlockSpec(memory_space=pl.ANY)
    dma = pltpu.SemaphoreType.DMA
    residual = pl.pallas_call(
        kernel,
        out_shape=jax.ShapeDtypeStruct((RB, PAIRS), jnp.float32),
        in_specs=[anywhere] * 5,
        out_specs=pl.BlockSpec(memory_space=pltpu.VMEM),
        scratch_shapes=[
            pltpu.SMEM(cd_tile.shape, jnp.int32),
            pltpu.SMEM(target.shape, jnp.int32),
            pltpu.SMEM(counts.shape, jnp.int32),
            pltpu.VMEM(amp.shape, jnp.bfloat16),
            pltpu.VMEM(integrals.shape, jnp.bfloat16),
            pltpu.VMEM((64, 128), jnp.float32),
            pltpu.VMEM((NY, NZ, 64, 128), jnp.bfloat16),
            pltpu.VMEM((NZ, NY, 64, 128), jnp.bfloat16),
            pltpu.VMEM((NZ * 64, 128), jnp.float32),
            pltpu.VMEM((KT, SLAB * SLABS, 128), jnp.float32),
            pltpu.VMEM((SLAB, KT * 128), jnp.bfloat16),
            pltpu.VMEM((SLAB * SLABS, SLAB * SLABS), jnp.bfloat16),
            pltpu.VMEM((SLAB * SLABS, 128), jnp.int32),
            pltpu.VMEM((SLABS, RB, SLAB), jnp.float32),
            pltpu.VMEM((3, SLABS, CODED, SLAB), jnp.int16),
            pltpu.VMEM((3, SLABS, CODED, SLAB), jnp.int16),
            dma((5,)),
            dma((11,)),
            dma((11,)),
            dma((2, 6, 2)),
            dma((2, 6, 2)),
            dma((12,)),
            dma((12,)),
            dma((SLABS, 3)),
            dma((SLABS, 3)),
        ],
        compiler_params=pltpu.CompilerParams(
            collective_id=0, has_side_effects=True, vmem_limit_bytes=56 * 1024 * 1024
        ),
        cost_estimate=pl.CostEstimate(flops=2 * SLOTS * RB * PAIRS * TP, bytes_accessed=6 * 10**6, transcendentals=0),
    )(cd_tile, target, counts, amp, integrals)
    return jnp.transpose(residual)[None]


def solution(mesh):
    in_specs = (P(None, "row", None), P(("row", "col"), None, None), P(), P(), P())
    out_specs = P(("row", "col"), None, None)
    return jax.shard_map(local, mesh=mesh, in_specs=in_specs, out_specs=out_specs, check_vma=False)
```

```python
import jax
import jax.numpy as jnp
from jax import lax
from jax.experimental import pallas as pl
from jax.experimental.pallas import tpu as pltpu
from jax.sharding import PartitionSpec as P

MESH = pl.DeviceIdType.MESH
NY, NZ, NX = 8, 12, 4
ROWS = 3
KT = 20
TP = 2500
CDW = 96
PAIRS = 576
RB = 200
SLOTS = 4
Y_REACH, Z_REACH = 2, 3
Z_NEAR, Y_NEAR = 5, 3
SLAB = 128
SLABS = 5
CODED = 208
FOLD, FOLDED = 104, 112
LEVELS = 32000.0
NT = (((1,), (1,)), ((), ()))


def block_order():
    order = []
    row = 0
    for half, index in (
        [(1, 0), (0, 0), (1, 1), (1, 2), (1, 3), (1, 4), (0, 1), (0, 2), (1, 5), (1, 6), (0, 3), (0, 4)]
        + [(1, 7), (1, 8), (0, 5), (0, 6), (1, 9), (1, 10), (1, 11), (0, 7)]
    ):
        order.append((half, index, row))
        row += 36 if half == 0 else 24
    return order


def slot_of(k, n):
    return 0 if k == 0 else 2 * k - 1 if k <= n // 2 else 2 * (n - k)


def distance(index):
    return -((index + 1) // 2) if index % 2 else index // 2


def kernel(
    cd_hbm, target_hbm, counts_hbm, amp_hbm, int_hbm, out_ref,
    cd_ref, target_ref, counts_ref, amp_v, int_v, shard_v, g0, g1, wide, a_f, a_b, perm, pidx,
    p_own, p_send, p_got,
    load_sem, p1_send, p1_recv, p2_send, p2_recv, sib_send, sib_recv, x_send, x_recv,
):
    row, col = lax.axis_index("row"), lax.axis_index("col")
    y, z, core = row // (2 * NZ), (row // 2) % NZ, row % 2

    def at(yy, zz, cc):
        return ((yy * NZ + zz) * 2 + cc, col)

    def along_y(k):
        return at((y + k + NY) % NY, z, core)

    def along_z(k):
        return at(y, (z + k + NZ) % NZ, core)

    sibling = at(y, z, 1 - core)
    def along_x(k):
        return (row, (col + k) % NX)


    load_amp = pltpu.make_async_copy(amp_hbm, amp_v, load_sem.at[0])
    load_int = pltpu.make_async_copy(int_hbm, int_v, load_sem.at[1])
    load_cd = pltpu.make_async_copy(cd_hbm, cd_ref, load_sem.at[2])
    load_target = pltpu.make_async_copy(target_hbm, target_ref, load_sem.at[3])
    load_counts = pltpu.make_async_copy(counts_hbm, counts_ref, load_sem.at[4])
    load_cd.start()
    load_amp.start()
    load_target.start()
    load_counts.start()

    barrier = pltpu.get_barrier_semaphore()

    def greet(others):
        for other in others:
            pl.semaphore_signal(barrier, inc=1, device_id=other, device_id_type=MESH)

    def reach(n, r):
        return [k for s in range(r, 0, -1) for k in (s, -s)]

    greet([sibling] + [along_x(k) for k in range(1, NX)])

    @pl.when(core == 0)
    def _():
        greet([along_z(k) for k in range(1, NZ)] + [along_y(k) for k in reach(NY, Y_REACH)])

    @pl.when(core == 1)
    def _():
        greet([along_y(k) for k in range(1, NY)] + [along_z(k) for k in reach(NZ, Z_REACH)])

    shard_v[...] = jnp.zeros_like(shard_v)
    load_cd.wait()
    apart = jnp.abs(lax.broadcasted_iota(jnp.int32, (16, CDW), 1) - cd_ref[col])
    one_hot = (1 - jnp.minimum(apart, 1)).astype(jnp.float32).astype(jnp.bfloat16)
    load_amp.wait()
    load_int.start()
    for p in range(ROWS):
        line = jnp.dot(one_hot, amp_v[p], preferred_element_type=jnp.float32)
        for k in range(KT):
            width = min(128, TP - 128 * k)
            shard_v[p * KT + k : p * KT + k + 1, 0:width] = line[0:1, 128 * k : 128 * k + width]
    packed = shard_v[...].astype(jnp.bfloat16)

    @pl.when(core == 0)
    def _():
        g0[y, 0] = packed
        pl.semaphore_wait(barrier, NX + NZ - 1 + 2 * Y_REACH)

    @pl.when(core == 1)
    def _():
        g1[z, 0] = packed
        pl.semaphore_wait(barrier, NX + NY - 1 + 2 * Z_REACH)

    def copy(src, dst, send, recv, device):
        return pltpu.make_async_remote_copy(
            src_ref=src, dst_ref=dst, send_sem=send, recv_sem=recv, device_id=device, device_id_type=MESH
        )

    def ring1(block, n, to):
        own, copies = block.at[0], {}
        for k in sorted(range(1, n), key=lambda k: min(k, n - k)):
            place = block.at[slot_of(n - k, n)]
            copies[k] = copy(own, place, p1_send.at[k - 1], p1_recv.at[k - 1], to(k))
            copies[k].start()
        return copies

    def ring2(buf, n, me, inner, near, far, to):
        def step(s, sign, piece):
            i, hop = (me, s) if s <= far else ((me - sign * far + n) % n, s - far)
            d = 0 if sign > 0 else 1
            ref = buf.at[i, pl.ds(0, near) if piece == 0 else pl.ds(near, inner - near)]
            return copy(ref, ref, p2_send.at[d, s - 1, piece], p2_recv.at[d, s - 1, piece], to(sign * hop))

        return step

    def pieces(n, s, sign):
        return (0, 1) if s < n // 2 else (0,) if sign > 0 else (1,)

    y_step = ring2(g0, NY, y, NZ, Z_NEAR, Y_REACH, along_y)
    z_step = ring2(g1, NZ, z, NY, Y_NEAR, Z_REACH, along_z)

    def block_at(half, index):
        n, me = (NY, y) if half == 0 else (NZ, z)
        return (me + distance(index) + n) % n

    def to_sibling(half, index):
        ref = (g0 if half == 0 else g1).at[block_at(half, index)]
        return copy(ref, ref, sib_send.at[index], sib_recv.at[index], sibling)

    def first(half):
        if half == 0:
            block, inner, to, step, n, far, near = g0.at[y], NZ, along_z, y_step, NY, Y_REACH, Z_NEAR
        else:
            block, inner, to, step, n, far, near = g1.at[z], NY, along_y, z_step, NZ, Z_REACH, Y_NEAR
        copies = ring1(block, inner, to)
        for piece in (0, 1):
            for k in range(1, inner):
                if (slot_of(inner - k, inner) < near) == (piece == 0):
                    copies[k].wait_recv()
            for s in range(far, 0, -1):
                for sign in (1, -1):
                    step(s, sign, piece).start()
        to_sibling(half, 0).start()
        for c in copies.values():
            c.wait_send()

    @pl.when(core == 0)
    def _():
        first(0)

    @pl.when(core == 1)
    def _():
        first(1)

    def second(half):
        n, step, far = (NY, y_step, Y_REACH) if half == 0 else (NZ, z_step, Z_REACH)
        for piece in (0, 1):
            for sign in (1, -1):
                step(far, sign, piece).wait_recv()
                for more in range(n // 2, far, -1):
                    if piece in pieces(n, more, sign):
                        step(more, sign, piece).start()
        for sign in (1, -1):
            to_sibling(half, 2 * far - (1 if sign > 0 else 0)).start()

    def arrive(half, s):
        n, step = (NY, y_step) if half == 0 else (NZ, z_step)

        @pl.when(core == half)
        def _():
            for sign in (1, -1):
                for piece in pieces(n, s, sign):
                    step(s, sign, piece).wait_recv()
                if s < n // 2:
                    to_sibling(half, 2 * s - (1 if sign > 0 else 0)).start()
            if s == n // 2:
                to_sibling(half, 2 * s - 1).start()

    load_target.wait()
    load_counts.wait()
    device = row * NX + col
    count = counts_ref[device]
    weights = []
    for d in range(NX):
        owner = (col + d) % NX
        line = []
        for q in range(SLOTS):
            live = jnp.minimum(jnp.maximum(count - q, 0), 1)
            same = 1 - jnp.minimum(jnp.abs(target_ref[device * SLOTS + q] - owner), 1)
            line.append((live * same).astype(jnp.float32))
        weights.append(line)

    order = block_order()
    pidx[...] = jnp.full_like(pidx, -1)
    for half, index, first_row in order:
        n, me = (NZ, z) if half == 0 else (NY, y)
        place = lax.broadcasted_iota(jnp.int32, (n, 128), 0)
        away = (place + 1) // 2
        source = me + jnp.where(place % 2 == 1, away, -away)
        source = jnp.where(source < 0, source + n, jnp.where(source >= n, source - n, source))
        for r in range(ROWS):
            if half == 0:
                pair = block_at(0, index) * 72 + source * 6 + r
            else:
                pair = source * 72 + block_at(1, index) * 6 + 3 + r
            pidx[first_row + n * r : first_row + n * r + n, :] = pair
    for t in range(SLABS):
        lanes = lax.broadcasted_iota(jnp.int32, (SLAB * SLABS, 128), 1) + 128 * t
        perm[:, 128 * t : 128 * t + 128] = jnp.where(pidx[...] == lanes, 1.0, 0.0).astype(jnp.bfloat16)
    a_f[:, PAIRS:, :] = jnp.zeros((KT, SLAB * SLABS - PAIRS, 128), jnp.float32)

    def unpack(half, index, first):
        n = NZ if half == 0 else NY
        i = block_at(half, index)

        @pl.when(core != half)
        def _():
            to_sibling(half, index).wait_recv()

        block = (g0 if half == 0 else g1)[i]
        wide[0 : n * 64, :] = block.reshape(n * 64, 128).astype(jnp.float32)

        @pl.loop(0, KT, unroll=5)
        def _(k):
            for r in range(ROWS):
                a_f[k, first + n * r : first + n * r + n, :] = wide[pl.ds(r * KT + k, n, stride=64), :]

    def x_copy(j, d):
        rows = pl.ds(0, CODED if j < SLABS - 1 else FOLDED)
        src, dst = p_send.at[d - 1, j, rows], p_got.at[d - 1, j, rows]
        return copy(src, dst, x_send.at[j, d - 1], x_recv.at[j, d - 1], along_x(d))

    def encode(part, j):
        top = jnp.maximum(jnp.max(jnp.abs(part), axis=0, keepdims=True), 2.0**-110)
        e = jnp.ceil(jnp.log2(top) * 64.0)
        codes = jnp.round(part * (jnp.exp2(e * (-1 / 64)) * LEVELS)).astype(jnp.int32)
        scale = jnp.broadcast_to(e.astype(jnp.int32), (CODED - RB, SLAB))
        if j == SLABS - 1:
            lower = pltpu.roll(codes[FOLD:], 64, 1)
            lower = jnp.concatenate([lower, jnp.zeros((2 * FOLD - RB, SLAB), jnp.int32)], axis=0)
            codes = codes[0:FOLD] + lower
        return jnp.concatenate([codes, scale], axis=0).astype(jnp.int16)

    def decode(d, j):
        if j < SLABS - 1:
            wide = p_got[d - 1, j].astype(jnp.int32)
            codes, e = wide[0:RB], wide[RB : RB + 1]
        else:
            wide = p_got[d - 1, j, 0:FOLDED].astype(jnp.int32)
            codes = jnp.concatenate([wide[0:FOLD], pltpu.roll(wide[0 : RB - FOLD], 64, 1)], axis=0)
            e = wide[FOLD : FOLD + 1]
        return codes.astype(jnp.float32) * (jnp.exp2(e.astype(jnp.float32) * (1 / 64)) * (1 / LEVELS))

    def slab(j):
        for k in range(KT):
            a_b[:, 128 * k : 128 * k + 128] = a_f[k, SLAB * j : SLAB * j + SLAB, :].astype(jnp.bfloat16)
        terms = [
            lax.dot_general(int_v[q], a_b[:, 0:TP], NT, preferred_element_type=jnp.float32) for q in range(SLOTS)
        ]

        def part(d):
            return sum(w * t for w, t in zip(weights[d], terms))

        for d in (2, 1, 3):
            coded = encode(part(d), j)
            p_send[d - 1, j, 0 : coded.shape[0]] = coded
            x_copy(j, d).start()
        p_own[j] = part(0)

    def finish(j):
        whole = p_own[j]
        for d in (1, 3, 2):
            x_copy(j, d).wait_recv()
            whole = whole + decode(d, j)
        high = whole.astype(jnp.bfloat16)
        low = (whole - high.astype(jnp.float32)).astype(jnp.bfloat16)
        mine = perm[SLAB * j : SLAB * j + SLAB, 0:PAIRS]
        more = jnp.dot(high, mine, preferred_element_type=jnp.float32)
        more = more + jnp.dot(low, mine, preferred_element_type=jnp.float32)
        if j == 0:
            out_ref[...] = more
        else:
            out_ref[...] = out_ref[...] + more

    at_row = {(h, i): f for h, i, f in order}

    def take(*blocks):
        for b in blocks:
            unpack(*b, at_row[b])

    @pl.when(core == 0)
    def _():
        second(0)

    @pl.when(core == 1)
    def _():
        second(1)

    take((1, 0), (0, 0))
    arrive(1, 2)
    arrive(0, 1)
    arrive(1, 1)
    take((1, 1), (1, 2), (1, 3), (1, 4))
    load_int.wait()
    slab(0)
    take((1, 5), (1, 6))
    take((0, 1), (0, 2))
    slab(1)
    arrive(1, 4)
    arrive(0, 3)
    take((0, 3), (0, 4))
    take((1, 7), (1, 8))
    slab(2)
    arrive(1, 5)
    arrive(1, 6)
    arrive(0, 4)
    take((0, 5), (0, 6))
    take((1, 9), (1, 10))
    slab(3)
    take((1, 11), (0, 7))
    slab(4)
    for j in range(SLABS):
        finish(j)

    def sent(n, step):
        for s in range(1, n // 2 + 1):
            for sign in (1, -1):
                for piece in pieces(n, s, sign):
                    step(s, sign, piece).wait_send()

    @pl.when(core == 0)
    def _():
        sent(NY, y_step)
        for index in range(NY):
            to_sibling(0, index).wait_send()

    @pl.when(core == 1)
    def _():
        sent(NZ, z_step)
        for index in range(NZ):
            to_sibling(1, index).wait_send()

    for j in range(SLABS):
        for d in range(1, NX):
            x_copy(j, d).wait_send()


def local(amplitudes, integrals, cd_tile, target, counts):
    amp = jnp.transpose(amplitudes, (1, 0, 2))
    anywhere = pl.BlockSpec(memory_space=pl.ANY)
    dma = pltpu.SemaphoreType.DMA
    residual = pl.pallas_call(
        kernel,
        out_shape=jax.ShapeDtypeStruct((RB, PAIRS), jnp.float32),
        in_specs=[anywhere] * 5,
        out_specs=pl.BlockSpec(memory_space=pltpu.VMEM),
        scratch_shapes=[
            pltpu.SMEM(cd_tile.shape, jnp.int32),
            pltpu.SMEM(target.shape, jnp.int32),
            pltpu.SMEM(counts.shape, jnp.int32),
            pltpu.VMEM(amp.shape, jnp.bfloat16),
            pltpu.VMEM(integrals.shape, jnp.bfloat16),
            pltpu.VMEM((64, 128), jnp.float32),
            pltpu.VMEM((NY, NZ, 64, 128), jnp.bfloat16),
            pltpu.VMEM((NZ, NY, 64, 128), jnp.bfloat16),
            pltpu.VMEM((NZ * 64, 128), jnp.float32),
            pltpu.VMEM((KT, SLAB * SLABS, 128), jnp.float32),
            pltpu.VMEM((SLAB, KT * 128), jnp.bfloat16),
            pltpu.VMEM((SLAB * SLABS, SLAB * SLABS), jnp.bfloat16),
            pltpu.VMEM((SLAB * SLABS, 128), jnp.int32),
            pltpu.VMEM((SLABS, RB, SLAB), jnp.float32),
            pltpu.VMEM((3, SLABS, CODED, SLAB), jnp.int16),
            pltpu.VMEM((3, SLABS, CODED, SLAB), jnp.int16),
            dma((5,)),
            dma((11,)),
            dma((11,)),
            dma((2, 6, 2)),
            dma((2, 6, 2)),
            dma((12,)),
            dma((12,)),
            dma((SLABS, 3)),
            dma((SLABS, 3)),
        ],
        compiler_params=pltpu.CompilerParams(
            collective_id=0, has_side_effects=True, vmem_limit_bytes=56 * 1024 * 1024
        ),
        cost_estimate=pl.CostEstimate(flops=2 * SLOTS * RB * PAIRS * TP, bytes_accessed=6 * 10**6, transcendentals=0),
    )(cd_tile, target, counts, amp, integrals)
    return jnp.transpose(residual)[None]


def solution(mesh):
    in_specs = (P(None, "row", None), P(("row", "col"), None, None), P(), P(), P())
    out_specs = P(("row", "col"), None, None)
    return jax.shard_map(local, mesh=mesh, in_specs=in_specs, out_specs=out_specs, check_vma=False)
```

```python
import jax
import jax.numpy as jnp
from jax import lax
from jax.experimental import pallas as pl
from jax.experimental.pallas import tpu as pltpu
from jax.sharding import PartitionSpec as P

MESH = pl.DeviceIdType.MESH
NY, NZ, NX = 8, 12, 4
ROWS = 3
KT = 20
TP = 2500
CDW = 96
PAIRS = 576
RB = 200
SLOTS = 4
Y_REACH, Z_REACH = 2, 3
Z_NEAR, Y_NEAR = 5, 3
SLAB = 128
SLABS = 5
CODED = 208
FOLD, FOLDED = 104, 112
LEVELS = 32000.0
NT = (((1,), (1,)), ((), ()))


def block_order():
    order = []
    row = 0
    for half, index in (
        [(1, 0), (0, 0), (1, 1), (1, 2), (1, 3), (1, 4), (0, 1), (0, 2), (1, 5), (1, 6), (0, 3), (0, 4)]
        + [(1, 7), (1, 8), (0, 5), (0, 6), (1, 9), (1, 10), (1, 11), (0, 7)]
    ):
        order.append((half, index, row))
        row += 36 if half == 0 else 24
    return order


def slot_of(k, n):
    return 0 if k == 0 else 2 * k - 1 if k <= n // 2 else 2 * (n - k)


def distance(index):
    return -((index + 1) // 2) if index % 2 else index // 2


def kernel(
    cd_hbm, target_hbm, counts_hbm, amp_hbm, int_hbm, out_ref,
    cd_ref, target_ref, counts_ref, amp_v, int_v, shard_v, g0, g1, wide, a_f, a_b, perm, pidx,
    p_own, p_send, p_got,
    load_sem, p1_send, p1_recv, p2_send, p2_recv, sib_send, sib_recv, x_send, x_recv,
):
    row, col = lax.axis_index("row"), lax.axis_index("col")
    y, z, core = row // (2 * NZ), (row // 2) % NZ, row % 2

    def at(yy, zz, cc):
        return ((yy * NZ + zz) * 2 + cc, col)

    def along_y(k):
        return at((y + k + NY) % NY, z, core)

    def along_z(k):
        return at(y, (z + k + NZ) % NZ, core)

    sibling = at(y, z, 1 - core)
    def along_x(k):
        return (row, (col + k) % NX)


    load_amp = pltpu.make_async_copy(amp_hbm, amp_v, load_sem.at[0])
    load_int = pltpu.make_async_copy(int_hbm, int_v, load_sem.at[1])
    load_cd = pltpu.make_async_copy(cd_hbm, cd_ref, load_sem.at[2])
    load_target = pltpu.make_async_copy(target_hbm, target_ref, load_sem.at[3])
    load_counts = pltpu.make_async_copy(counts_hbm, counts_ref, load_sem.at[4])
    load_cd.start()
    load_amp.start()
    load_target.start()
    load_counts.start()

    barrier = pltpu.get_barrier_semaphore()

    def greet(others):
        for other in others:
            pl.semaphore_signal(barrier, inc=1, device_id=other, device_id_type=MESH)

    def reach(n, r):
        return [k for s in range(r, 0, -1) for k in (s, -s)]

    greet([sibling] + [along_x(k) for k in range(1, NX)])

    @pl.when(core == 0)
    def _():
        greet([along_z(k) for k in range(1, NZ)] + [along_y(k) for k in reach(NY, Y_REACH)])

    @pl.when(core == 1)
    def _():
        greet([along_y(k) for k in range(1, NY)] + [along_z(k) for k in reach(NZ, Z_REACH)])

    shard_v[...] = jnp.zeros_like(shard_v)
    load_cd.wait()
    apart = jnp.abs(lax.broadcasted_iota(jnp.int32, (16, CDW), 1) - cd_ref[col])
    one_hot = (1 - jnp.minimum(apart, 1)).astype(jnp.float32).astype(jnp.bfloat16)
    load_amp.wait()
    load_int.start()
    for p in range(ROWS):
        line = jnp.dot(one_hot, amp_v[p], preferred_element_type=jnp.float32)
        for k in range(KT):
            width = min(128, TP - 128 * k)
            shard_v[p * KT + k : p * KT + k + 1, 0:width] = line[0:1, 128 * k : 128 * k + width]
    packed = shard_v[...].astype(jnp.bfloat16)

    @pl.when(core == 0)
    def _():
        g0[y, 0] = packed
        pl.semaphore_wait(barrier, NX + NZ - 1 + 2 * Y_REACH)

    @pl.when(core == 1)
    def _():
        g1[z, 0] = packed
        pl.semaphore_wait(barrier, NX + NY - 1 + 2 * Z_REACH)

    def copy(src, dst, send, recv, device):
        return pltpu.make_async_remote_copy(
            src_ref=src, dst_ref=dst, send_sem=send, recv_sem=recv, device_id=device, device_id_type=MESH
        )

    def ring1(block, n, to):
        own, copies = block.at[0], {}
        for k in sorted(range(1, n), key=lambda k: min(k, n - k)):
            place = block.at[slot_of(n - k, n)]
            copies[k] = copy(own, place, p1_send.at[k - 1], p1_recv.at[k - 1], to(k))
            copies[k].start()
        return copies

    def ring2(buf, n, me, inner, near, far, to):
        def step(s, sign, piece):
            i, hop = (me, s) if s <= far else ((me - sign * far + n) % n, s - far)
            d = 0 if sign > 0 else 1
            ref = buf.at[i, pl.ds(0, near) if piece == 0 else pl.ds(near, inner - near)]
            return copy(ref, ref, p2_send.at[d, s - 1, piece], p2_recv.at[d, s - 1, piece], to(sign * hop))

        return step

    def pieces(n, s, sign):
        return (0, 1) if s < n // 2 else (0,) if sign > 0 else (1,)

    y_step = ring2(g0, NY, y, NZ, Z_NEAR, Y_REACH, along_y)
    z_step = ring2(g1, NZ, z, NY, Y_NEAR, Z_REACH, along_z)

    def block_at(half, index):
        n, me = (NY, y) if half == 0 else (NZ, z)
        return (me + distance(index) + n) % n

    def to_sibling(half, index):
        ref = (g0 if half == 0 else g1).at[block_at(half, index)]
        return copy(ref, ref, sib_send.at[index], sib_recv.at[index], sibling)

    def first(half):
        if half == 0:
            block, inner, to, step, n, far, near = g0.at[y], NZ, along_z, y_step, NY, Y_REACH, Z_NEAR
        else:
            block, inner, to, step, n, far, near = g1.at[z], NY, along_y, z_step, NZ, Z_REACH, Y_NEAR
        copies = ring1(block, inner, to)
        for piece in (0, 1):
            for k in range(1, inner):
                if (slot_of(inner - k, inner) < near) == (piece == 0):
                    copies[k].wait_recv()
            for s in range(far, 0, -1):
                for sign in (1, -1):
                    step(s, sign, piece).start()
        to_sibling(half, 0).start()
        for c in copies.values():
            c.wait_send()

    @pl.when(core == 0)
    def _():
        first(0)

    @pl.when(core == 1)
    def _():
        first(1)

    def second(half):
        n, step, far = (NY, y_step, Y_REACH) if half == 0 else (NZ, z_step, Z_REACH)
        for piece in (0, 1):
            for sign in (1, -1):
                step(far, sign, piece).wait_recv()
                for more in range(n // 2, far, -1):
                    if piece in pieces(n, more, sign):
                        step(more, sign, piece).start()
        for sign in (1, -1):
            to_sibling(half, 2 * far - (1 if sign > 0 else 0)).start()

    def arrive(half, s):
        n, step = (NY, y_step) if half == 0 else (NZ, z_step)

        @pl.when(core == half)
        def _():
            for sign in (1, -1):
                for piece in pieces(n, s, sign):
                    step(s, sign, piece).wait_recv()
                if s < n // 2:
                    to_sibling(half, 2 * s - (1 if sign > 0 else 0)).start()
            if s == n // 2:
                to_sibling(half, 2 * s - 1).start()

    load_target.wait()
    load_counts.wait()
    device = row * NX + col
    count = counts_ref[device]
    weights = []
    for d in range(NX):
        owner = (col + d) % NX
        line = []
        for q in range(SLOTS):
            live = jnp.minimum(jnp.maximum(count - q, 0), 1)
            same = 1 - jnp.minimum(jnp.abs(target_ref[device * SLOTS + q] - owner), 1)
            line.append((live * same).astype(jnp.float32))
        weights.append(line)

    order = block_order()
    pidx[...] = jnp.full_like(pidx, -1)
    for half, index, first_row in order:
        n, me = (NZ, z) if half == 0 else (NY, y)
        place = lax.broadcasted_iota(jnp.int32, (n, 128), 0)
        away = (place + 1) // 2
        source = me + jnp.where(place % 2 == 1, away, -away)
        source = jnp.where(source < 0, source + n, jnp.where(source >= n, source - n, source))
        for r in range(ROWS):
            if half == 0:
                pair = block_at(0, index) * 72 + source * 6 + r
            else:
                pair = source * 72 + block_at(1, index) * 6 + 3 + r
            pidx[first_row + n * r : first_row + n * r + n, :] = pair
    for t in range(SLABS):
        lanes = lax.broadcasted_iota(jnp.int32, (SLAB * SLABS, 128), 1) + 128 * t
        perm[:, 128 * t : 128 * t + 128] = jnp.where(pidx[...] == lanes, 1.0, 0.0).astype(jnp.bfloat16)
    a_f[:, PAIRS:, :] = jnp.zeros((KT, SLAB * SLABS - PAIRS, 128), jnp.float32)

    def unpack(half, index, first):
        n = NZ if half == 0 else NY
        i = block_at(half, index)

        @pl.when(core != half)
        def _():
            to_sibling(half, index).wait_recv()

        block = (g0 if half == 0 else g1)[i]
        wide[0 : n * 64, :] = block.reshape(n * 64, 128).astype(jnp.float32)

        @pl.loop(0, KT, unroll=10)
        def _(k):
            for r in range(ROWS):
                a_f[k, first + n * r : first + n * r + n, :] = wide[pl.ds(r * KT + k, n, stride=64), :]

    def x_copy(j, d):
        rows = pl.ds(0, CODED if j < SLABS - 1 else FOLDED)
        src, dst = p_send.at[d - 1, j, rows], p_got.at[d - 1, j, rows]
        return copy(src, dst, x_send.at[j, d - 1], x_recv.at[j, d - 1], along_x(d))

    def encode(part, j):
        top = jnp.maximum(jnp.max(jnp.abs(part), axis=0, keepdims=True), 2.0**-110)
        e = jnp.ceil(jnp.log2(top) * 64.0)
        codes = jnp.round(part * (jnp.exp2(e * (-1 / 64)) * LEVELS)).astype(jnp.int32)
        scale = jnp.broadcast_to(e.astype(jnp.int32), (CODED - RB, SLAB))
        if j == SLABS - 1:
            lower = pltpu.roll(codes[FOLD:], 64, 1)
            lower = jnp.concatenate([lower, jnp.zeros((2 * FOLD - RB, SLAB), jnp.int32)], axis=0)
            codes = codes[0:FOLD] + lower
        return jnp.concatenate([codes, scale], axis=0).astype(jnp.int16)

    def decode(d, j):
        if j < SLABS - 1:
            wide = p_got[d - 1, j].astype(jnp.int32)
            codes, e = wide[0:RB], wide[RB : RB + 1]
        else:
            wide = p_got[d - 1, j, 0:FOLDED].astype(jnp.int32)
            codes = jnp.concatenate([wide[0:FOLD], pltpu.roll(wide[0 : RB - FOLD], 64, 1)], axis=0)
            e = wide[FOLD : FOLD + 1]
        return codes.astype(jnp.float32) * (jnp.exp2(e.astype(jnp.float32) * (1 / 64)) * (1 / LEVELS))

    def slab(j):
        for k in range(KT):
            a_b[:, 128 * k : 128 * k + 128] = a_f[k, SLAB * j : SLAB * j + SLAB, :].astype(jnp.bfloat16)
        terms = [
            lax.dot_general(int_v[q], a_b[:, 0:TP], NT, preferred_element_type=jnp.float32) for q in range(SLOTS)
        ]

        def part(d):
            return sum(w * t for w, t in zip(weights[d], terms))

        for d in (2, 1, 3):
            coded = encode(part(d), j)
            p_send[d - 1, j, 0 : coded.shape[0]] = coded
            x_copy(j, d).start()
        p_own[j] = part(0)

    def finish(j):
        whole = p_own[j]
        for d in (1, 3, 2):
            x_copy(j, d).wait_recv()
            whole = whole + decode(d, j)
        high = whole.astype(jnp.bfloat16)
        low = (whole - high.astype(jnp.float32)).astype(jnp.bfloat16)
        mine = perm[SLAB * j : SLAB * j + SLAB, 0:PAIRS]
        more = jnp.dot(high, mine, preferred_element_type=jnp.float32)
        more = more + jnp.dot(low, mine, preferred_element_type=jnp.float32)
        if j == 0:
            out_ref[...] = more
        else:
            out_ref[...] = out_ref[...] + more

    at_row = {(h, i): f for h, i, f in order}

    def take(*blocks):
        for b in blocks:
            unpack(*b, at_row[b])

    @pl.when(core == 0)
    def _():
        second(0)

    @pl.when(core == 1)
    def _():
        second(1)

    take((1, 0), (0, 0))
    arrive(1, 2)
    arrive(0, 1)
    arrive(1, 1)
    take((1, 1), (1, 2), (1, 3), (1, 4))
    load_int.wait()
    slab(0)
    take((0, 1), (0, 2))
    take((1, 5), (1, 6))
    slab(1)
    arrive(1, 4)
    arrive(0, 3)
    take((0, 3), (0, 4))
    take((1, 7), (1, 8))
    slab(2)
    arrive(1, 5)
    arrive(1, 6)
    arrive(0, 4)
    take((0, 5), (0, 6))
    take((1, 9), (1, 10))
    slab(3)
    take((1, 11), (0, 7))
    slab(4)
    for j in range(SLABS):
        finish(j)

    def sent(n, step):
        for s in range(1, n // 2 + 1):
            for sign in (1, -1):
                for piece in pieces(n, s, sign):
                    step(s, sign, piece).wait_send()

    @pl.when(core == 0)
    def _():
        sent(NY, y_step)
        for index in range(NY):
            to_sibling(0, index).wait_send()

    @pl.when(core == 1)
    def _():
        sent(NZ, z_step)
        for index in range(NZ):
            to_sibling(1, index).wait_send()

    for j in range(SLABS):
        for d in range(1, NX):
            x_copy(j, d).wait_send()


def local(amplitudes, integrals, cd_tile, target, counts):
    amp = jnp.transpose(amplitudes, (1, 0, 2))
    anywhere = pl.BlockSpec(memory_space=pl.ANY)
    dma = pltpu.SemaphoreType.DMA
    residual = pl.pallas_call(
        kernel,
        out_shape=jax.ShapeDtypeStruct((RB, PAIRS), jnp.float32),
        in_specs=[anywhere] * 5,
        out_specs=pl.BlockSpec(memory_space=pltpu.VMEM),
        scratch_shapes=[
            pltpu.SMEM(cd_tile.shape, jnp.int32),
            pltpu.SMEM(target.shape, jnp.int32),
            pltpu.SMEM(counts.shape, jnp.int32),
            pltpu.VMEM(amp.shape, jnp.bfloat16),
            pltpu.VMEM(integrals.shape, jnp.bfloat16),
            pltpu.VMEM((64, 128), jnp.float32),
            pltpu.VMEM((NY, NZ, 64, 128), jnp.bfloat16),
            pltpu.VMEM((NZ, NY, 64, 128), jnp.bfloat16),
            pltpu.VMEM((NZ * 64, 128), jnp.float32),
            pltpu.VMEM((KT, SLAB * SLABS, 128), jnp.float32),
            pltpu.VMEM((SLAB, KT * 128), jnp.bfloat16),
            pltpu.VMEM((SLAB * SLABS, SLAB * SLABS), jnp.bfloat16),
            pltpu.VMEM((SLAB * SLABS, 128), jnp.int32),
            pltpu.VMEM((SLABS, RB, SLAB), jnp.float32),
            pltpu.VMEM((3, SLABS, CODED, SLAB), jnp.int16),
            pltpu.VMEM((3, SLABS, CODED, SLAB), jnp.int16),
            dma((5,)),
            dma((11,)),
            dma((11,)),
            dma((2, 6, 2)),
            dma((2, 6, 2)),
            dma((12,)),
            dma((12,)),
            dma((SLABS, 3)),
            dma((SLABS, 3)),
        ],
        compiler_params=pltpu.CompilerParams(
            collective_id=0, has_side_effects=True, vmem_limit_bytes=56 * 1024 * 1024
        ),
        cost_estimate=pl.CostEstimate(flops=2 * SLOTS * RB * PAIRS * TP, bytes_accessed=6 * 10**6, transcendentals=0),
    )(cd_tile, target, counts, amp, integrals)
    return jnp.transpose(residual)[None]


def solution(mesh):
    in_specs = (P(None, "row", None), P(("row", "col"), None, None), P(), P(), P())
    out_specs = P(("row", "col"), None, None)
    return jax.shard_map(local, mesh=mesh, in_specs=in_specs, out_specs=out_specs, check_vma=False)
```
